256 devices in a mesh: tm: 16 (over x_hi, y, core), space: 16 (over z, x_lo).
Axes of the slice: x: 4 (x_hi: 2, x_lo: 2; x = x_hi * 2 + x_lo), y: 4, z: 8, core: 2. Of those that a mesh axis runs over, the one named last changes fastest.
Arguments:
- queries: bfloat16 [16, 16, 128, 1536], P('tm', 'space'), may hold values from -100 to 100
- key_states: bfloat16 [16, 16, 128, 1536], P('tm', 'space'), may hold values from -4.5 to 4.5
- value_states: bfloat16 [16, 16, 128, 1536], P('tm', 'space'), may hold values from -6 to 6
- grad_out: bfloat16 [16, 16, 128, 1536], P('tm', 'space'), may hold values from -6 to 6
- window: int32 [16, 16, 2, 27], P('tm', 'space'), may hold values 0 or 1
Outputs:
- grad_queries: bfloat16 [16, 16, 128, 1536], P('tm', 'space')
- grad_keys: bfloat16 [16, 16, 128, 1536], P('tm', 'space')
- grad_values: bfloat16 [16, 16, 128, 1536], P('tm', 'space')
The draws below stay inside these ranges and needn't reach their ends.
All inputs are finite; a program needn't handle non-finite values. No bound on the sum of `window` on one device may be relied on, other than what follows from the above.
Results may differ from the reference program's by a relative error of at most 0.011.
Values may be sent and summed in bfloat16 or wider, within the bound.
A program may use at most 64 MiB of HBM per device.

```python
import jax
import jax.numpy as jnp
from jax import lax

HEADS = 12
HEAD_DIM = 128
FEATURES = 1536
TILE_TOKENS = 64
COL_TILES = 2
BLOCK_TOKENS = 128
SLABS = 16
BANDS = 16


def shared_keys(key):
    raw = jax.random.normal(key, (SLABS, BANDS, BLOCK_TOKENS, FEATURES), jnp.float32)
    return jnp.clip(raw, -4.5, 4.5)


def draw_key_states(key, part):
    base = shared_keys(key)
    return base.astype(jnp.bfloat16)


def draw_queries(key, part):
    key = jax.random.fold_in(key, 2)
    fresh = jnp.clip(jax.random.normal(key, (SLABS, BANDS, BLOCK_TOKENS, FEATURES), jnp.float32), -4.5, 4.5)
    return fresh.astype(jnp.bfloat16)


def touch_ends(drawn, key, low, largest):
    index_at = [jax.random.randint(jax.random.fold_in(key, axis), (), 0, length) for axis, length in enumerate(drawn.shape)]
    main_axis = drawn.shape.index(max(drawn.shape))
    beside = index_at[:main_axis] + [(index_at[main_axis] + 1) % drawn.shape[main_axis]] + index_at[main_axis + 1:]
    return drawn.at[tuple(index_at)].set(low).at[tuple(beside)].set(largest)


def block_scale(rng, shape, cuts, least, high):
    loudness, own = 1.0, jax.random.fold_in(rng, 6)
    for axis_at, shards_of in cuts:
        draws = jnp.exp(jax.random.uniform(jax.random.fold_in(own, axis_at), (shards_of,), jnp.float32, least / len(cuts), high / len(cuts)))
        loudness = loudness * jnp.repeat(draws, shape[axis_at] // shards_of).reshape([-1 if axis == axis_at else 1 for axis in range(len(shape))])
    return loudness


def scatter_about(rng, shape, width, reach, cuts=(), kind=jnp.bfloat16):
    result = width * jax.random.normal(rng, shape, jnp.float32)
    if cuts:
        result = result * block_scale(rng, shape, cuts, -0.22, 0.18)
    return jnp.clip(result, -reach, reach).astype(kind)


def setup_inputs(seed: int = 0) -> dict:
    streams_of = jax.random.split(jax.random.key(seed), 6)
    return {
        "queries": draw_queries(jax.random.fold_in(streams_of[5], 71), 0),
        "key_states": draw_key_states(jax.random.fold_in(streams_of[5], 71), 0),
        "value_states": scatter_about(streams_of[2], (SLABS, BANDS, BLOCK_TOKENS, FEATURES), 1.0, 6.0, ((0, 16), (1, 16))),
        "grad_out": scatter_about(streams_of[3], (SLABS, BANDS, BLOCK_TOKENS, FEATURES), 1.0, 6.0, ((0, 16), (1, 16))),
        "window": touch_ends((jax.random.randint(streams_of[4], (SLABS, BANDS, COL_TILES, 27), 0, 3) < 2).astype(jnp.int32), jax.random.fold_in(streams_of[4], 1), 0, 1),
    }


CROSS = ((0, 1), (1, 0), (1, 1), (1, 2), (2, 1))


def split_heads(token_rows):
    return token_rows.reshape(token_rows.shape[0], HEADS, HEAD_DIM).astype(jnp.float32)


def inside(position, offset_step, extent):
    return (position + offset_step >= 0) & (position + offset_step < extent)


def tile_allow(listed, frame_step, band_step, present):
    tile_count = listed.shape[0]
    query_tile = jnp.arange(tile_count)[:, None]
    key_tile = jnp.arange(tile_count)[None, :]
    column_step = key_tile - query_tile
    offset_code = (frame_step + 1) * 9 + (band_step + 1) * 3 + jnp.clip(column_step, -1, 1) + 1
    onehot = offset_code[:, :, None] == jnp.arange(27)[None, None, :]
    chosen = jnp.sum(jnp.where(onehot, listed[:, None, :], 0), axis=2) > 0
    centre = (frame_step == 0) & (band_step == 0) & (column_step == 0)
    return present & (jnp.abs(column_step) <= 1) & (chosen | centre)


def expand(allowed):
    return jnp.repeat(jnp.repeat(allowed, TILE_TOKENS, axis=0), TILE_TOKENS, axis=1)


def reference(queries, key_states, value_states, grad_out, window):
    slab_count, band_count, block_rows, feature_count = queries.shape
    score_scale = HEAD_DIM ** -0.5
    packed = jnp.concatenate([key_states, value_states], axis=3)
    padded = jnp.pad(packed, ((1, 1), (1, 1), (0, 0), (0, 0)))
    zero_index = jnp.zeros((), jnp.int32)

    def visit(totals, visit_index):
        slab_index = (visit_index // band_count).astype(jnp.int32)
        band_index = (visit_index % band_count).astype(jnp.int32)
        start = (slab_index, band_index, zero_index, zero_index)
        nearby = lax.dynamic_slice(padded, start, (3, 3, block_rows, 2 * feature_count))
        chosen_blocks = jnp.stack([nearby[f, b] for f, b in CROSS])
        key_heads = split_heads(chosen_blocks[:, :, :feature_count].reshape(5 * block_rows, feature_count))
        value_heads = split_heads(chosen_blocks[:, :, feature_count:].reshape(5 * block_rows, feature_count))
        query_heads = split_heads(lax.dynamic_slice(queries, start, (1, 1, block_rows, feature_count))[0, 0])
        grad_heads = split_heads(lax.dynamic_slice(grad_out, start, (1, 1, block_rows, feature_count))[0, 0])
        listed = lax.dynamic_slice(window, start, (1, 1, window.shape[2], window.shape[3]))[0, 0]
        pieces = []
        for frame_pos, band_pos in CROSS:
            present = inside(slab_index, frame_pos - 1, slab_count) & inside(band_index, band_pos - 1, band_count)
            pieces.append(tile_allow(listed, frame_pos - 1, band_pos - 1, present))
        allowed = expand(jnp.concatenate(pieces, axis=1))
        scores = jnp.einsum("qhd,khd->hqk", query_heads, key_heads) * score_scale
        scores = jnp.where(allowed[None], scores, -1e30)
        row_top = jnp.max(scores, axis=2, keepdims=True)
        weight = jnp.exp(scores - row_top)
        row_total = jnp.sum(weight, axis=2, keepdims=True)
        prob_full = weight / row_total
        prob_low = prob_full.astype(jnp.bfloat16).astype(jnp.float32)
        attended = jnp.einsum("hqk,khd->qhd", prob_low, value_heads)
        row_delta = jnp.sum(grad_heads * attended, axis=2).T[:, :, None]
        grad_probs = jnp.einsum("qhd,khd->hqk", grad_heads, value_heads)
        grad_scores = (prob_full * (grad_probs - row_delta) * score_scale).astype(jnp.bfloat16).astype(jnp.float32)
        query_grad = jnp.einsum("hqk,khd->qhd", grad_scores, key_heads).reshape(block_rows, feature_count)
        key_grad = jnp.einsum("hqk,qhd->khd", grad_scores, query_heads).reshape(5, block_rows, feature_count)
        value_grad = jnp.einsum("hqk,qhd->khd", prob_low, grad_heads).reshape(5, block_rows, feature_count)
        partial_value = jnp.concatenate([key_grad, value_grad], axis=2)
        for place in range(5):
            frame_pos, band_pos = CROSS[place]
            spot = (slab_index + frame_pos, band_index + band_pos, zero_index, zero_index)
            current = lax.dynamic_slice(totals, spot, (1, 1, block_rows, 2 * feature_count))
            totals = lax.dynamic_update_slice(totals, current + partial_value[place][None, None], spot)
        return totals, query_grad.astype(jnp.bfloat16)

    first = jnp.zeros((slab_count + 2, band_count + 2, block_rows, 2 * feature_count), jnp.float32)
    totals, query_grads = lax.scan(visit, first, jnp.arange(slab_count * band_count, dtype=jnp.int32))
    grad_queries = query_grads.reshape(slab_count, band_count, block_rows, feature_count)
    interior = totals[1:-1, 1:-1]
    grad_keys = interior[:, :, :, :feature_count].astype(jnp.bfloat16)
    grad_values = interior[:, :, :, feature_count:].astype(jnp.bfloat16)
    return (grad_queries, grad_keys, grad_values)
```

```python
import functools
import math

import jax
import jax.numpy as jnp
from jax import lax
from jax.experimental import pallas as pl
from jax.experimental.pallas import tpu as pltpu
from jax.sharding import PartitionSpec as P

MESH = pl.DeviceIdType.MESH
HEAD_DIM = 128
TILE_TOKENS = 64
BLOCK = 128
MASKED = -1e30
SCALE = HEAD_DIM ** (-0.5)
SCALE_LOG2E = SCALE * math.log2(math.e)

OWN, C, Y, X, F = range(5)
GROUP = 2
LAG_PHASE1, LAG_COMBINE, LAG_PHASE2, LAG_XRET, LAG_FINAL = 1, 2, 3, 4, 5


def kernel(
    slabs,
    bands,
    chunks,
    q_hbm,
    k_hbm,
    v_hbm,
    g_hbm,
    window,
    dq_out,
    dk_out,
    dv_out,
    k_ref,
    v_ref,
    qd,
    weight,
    gprob,
    bias_out,
    bias_in,
    st_own,
    st_out,
    st_in,
    fin_own,
    fin_out,
    fin_in,
    dq_own,
    dq_send,
    dq_in,
    load_sem,
    bias_ssem,
    bias_rsem,
    fwd_ssem,
    fwd_rsem,
    st_ssem,
    st_rsem,
    fin_ssem,
    fin_rsem,
    dq_ssem,
    dq_rsem,
):
    t = lax.axis_index("tm")
    b = lax.axis_index("space")
    todd = lax.rem(t, 2)
    bodd = lax.rem(b, 2)
    tstep = 2 * todd - 1
    bstep = 1 - 2 * bodd
    t_c = t - tstep
    t_y = t + tstep
    b_x = b + bstep
    b_f = b - bstep
    b_zout = b + 2 * bstep
    b_zin = b - 2 * bstep
    has_y = (t_y >= 0) & (t_y < slabs)
    has_f = (b_f >= 0) & (b_f < bands)
    has_zout = (b_zout >= 0) & (b_zout < bands)
    bent = (t == slabs // 2 - 1) | (t == slabs // 2)
    straight = has_y & jnp.logical_not(bent)
    b_y = jnp.where(bent, b_x, b)

    partner = {C: (t_c, b), Y: (t_y, b), X: (t, b_x), F: (t, b_f)}
    present = {C: None, Y: has_y, X: None, F: has_f}
    bulk_y = (t_y, b_y)
    zout, zin = (t, b_zout), (t, b_zin)

    def guarded(condition, action):
        if condition is None:
            action()
        else:
            pl.when(condition)(action)

    def load_chunk(c, which):
        src = (q_hbm, g_hbm)[which]
        cols = pl.ds(pl.multiple_of(c * GROUP * HEAD_DIM, GROUP * HEAD_DIM), GROUP * HEAD_DIM)
        return pltpu.make_async_copy(
            src.at[0, 0, :, cols], qd.at[OWN, c, which], load_sem.at[which, c]
        )

    k_load = pltpu.make_async_copy(k_hbm.at[0, 0], k_ref, load_sem.at[2, 0])
    v_load = pltpu.make_async_copy(v_hbm.at[0, 0], v_ref, load_sem.at[2, 1])

    @pl.loop(0, chunks)
    def _(c):
        load_chunk(c, 0).start()
        load_chunk(c, 1).start()

    k_load.start()
    v_load.start()

    barrier = pltpu.get_barrier_semaphore()

    def greet(device):
        pl.semaphore_signal(barrier, inc=1, device_id=device, device_id_type=MESH)

    for n in (C, Y, X, F):
        guarded(present[n], functools.partial(greet, partner[n]))
    guarded(bent, functools.partial(greet, bulk_y))
    guarded(has_zout, functools.partial(greet, zout))
    guarded(has_f, functools.partial(greet, zin))

    lane_tile = lax.broadcasted_iota(jnp.int32, (1, BLOCK), 1) // TILE_TOKENS
    dirs = {
        OWN: (0, 0),
        C: (-tstep, 0),
        Y: (tstep, 0),
        X: (0, bstep),
        F: (0, -bstep),
    }
    for n in (OWN, C, Y, X, F):
        dt, dr = dirs[n]
        for key_tile in range(2):
            row = None
            for query_tile in range(2):
                dc = key_tile - query_tile
                if n == OWN and dc == 0:
                    value = jnp.float32(0.0)
                else:
                    code = 9 * (dt + 1) + 3 * (dr + 1) + dc + 1
                    listed = window[0, 0, query_tile, code]
                    value = jnp.where(listed == 1, 0.0, MASKED).astype(jnp.float32)
                part = jnp.full((1, BLOCK), value, jnp.float32)
                row = part if row is None else jnp.where(lane_tile == 0, row, part)
            if n == OWN:
                bias_in[OWN, key_tile] = row
            else:
                bias_out[n, key_tile] = row

    def blank(n):
        bias_in[n] = jnp.zeros_like(bias_in[n])

        @pl.loop(0, chunks)
        def _(c):
            qd[n, c] = jnp.zeros(qd.shape[2:], qd.dtype)
            for g in range(GROUP):
                st_in[n, c, 3 * g] = jnp.full((1, BLOCK), MASKED, jnp.float32)
                st_in[n, c, 3 * g + 1] = jnp.zeros((1, BLOCK), jnp.float32)
                st_in[n, c, 3 * g + 2] = jnp.zeros((1, BLOCK), jnp.float32)
                fin_in[n, c, 2 * g] = jnp.zeros((1, BLOCK), jnp.float32)
                fin_in[n, c, 2 * g + 1] = jnp.zeros((1, BLOCK), jnp.float32)
            if n != F:
                dq_in[n, c] = jnp.zeros(dq_in.shape[2:], dq_in.dtype)

    pl.when(jnp.logical_not(has_y))(functools.partial(blank, Y))
    pl.when(jnp.logical_not(has_f))(functools.partial(blank, F))

    @pl.when(jnp.logical_not(has_zout))
    def _():
        @pl.loop(0, chunks)
        def _(c):
            dq_in[F, c] = jnp.zeros(dq_in.shape[2:], dq_in.dtype)

    count = 2 + 2 * has_f.astype(jnp.int32) + has_y.astype(jnp.int32)
    count = count + bent.astype(jnp.int32) + has_zout.astype(jnp.int32)
    pl.semaphore_wait(barrier, count)

    def remote(src, dst, send, recv, device):
        return pltpu.make_async_remote_copy(
            src_ref=src,
            dst_ref=dst,
            send_sem=send,
            recv_sem=recv,
            device_id=device,
            device_id_type=MESH,
        )

    def bias_copy(n):
        return remote(
            bias_out.at[n], bias_in.at[n], bias_ssem.at[n], bias_rsem.at[n], partner[n]
        )

    def forward(n, c):
        return remote(
            qd.at[OWN, c], qd.at[n, c], fwd_ssem.at[n, c], fwd_rsem.at[n, c], partner[n]
        )

    def bent_forward(c):
        return remote(qd.at[X, c], qd.at[Y, c], fwd_ssem.at[Y, c], fwd_rsem.at[Y, c], bulk_y)

    def relay(c):
        return remote(qd.at[X, c], qd.at[F, c], fwd_ssem.at[F, c], fwd_rsem.at[F, c], zout)

    def st_copy(n, c):
        return remote(
            st_out.at[n, c], st_in.at[n, c], st_ssem.at[n, c], st_rsem.at[n, c], partner[n]
        )

    def fin_copy(n, c):
        return remote(
            fin_out.at[n, c], fin_in.at[n, c], fin_ssem.at[n, c], fin_rsem.at[n, c], partner[n]
        )

    def dq_copy(n, c):
        device = {C: partner[C], Y: bulk_y, X: partner[X], F: zin}[n]
        return remote(
            dq_send.at[n, c], dq_in.at[n, c], dq_ssem.at[n, c], dq_rsem.at[n, c], device
        )

    for n in (X, F, C, Y):
        guarded(present[n], lambda n=n: bias_copy(n).start())

    @pl.loop(0, chunks)
    def _(c):
        load_chunk(c, 0).wait()
        load_chunk(c, 1).wait()
        forward(X, c).start()
        forward(C, c).start()

        @pl.when(straight)
        def _():
            forward(Y, c).start()

    k_load.wait()
    v_load.wait()
    for n in (X, F, C, Y):
        guarded(present[n], lambda n=n: bias_copy(n).wait_recv())

    def head_cols(c, g):
        return pl.ds(pl.multiple_of((c * GROUP + g) * HEAD_DIM, HEAD_DIM), HEAD_DIM)

    def nearby(c, which, g):
        cols = slice(g * HEAD_DIM, (g + 1) * HEAD_DIM)
        return jnp.concatenate([qd[n, c, which, :, cols] for n in range(5)], axis=0)

    def stage_relay(c):
        forward(X, c).wait_recv()

        @pl.when(has_zout)
        def _():
            relay(c).start()

        @pl.when(bent)
        def _():
            bent_forward(c).start()

    def stage_phase1(c):
        forward(C, c).wait_recv()

        @pl.when(has_y)
        def _():
            forward(Y, c).wait_recv()

        @pl.when(has_f)
        def _():
            relay(c).wait_recv()

        masks = jnp.concatenate(
            [
                jnp.concatenate([bias_in[n, key_tile] for n in range(5)], axis=1)
                for key_tile in range(2)
            ],
            axis=0,
        )
        for g in range(GROUP):
            keys = k_ref[:, head_cols(c, g)]
            values = v_ref[:, head_cols(c, g)]
            contract = (((1,), (1,)), ((), ()))
            scores = lax.dot_general(
                keys, nearby(c, 0, g), contract, preferred_element_type=jnp.float32
            )
            scores = jnp.concatenate(
                [scores[:TILE_TOKENS] + masks[0:1], scores[TILE_TOKENS:] + masks[1:2]], axis=0
            )
            top = jnp.max(scores, axis=0, keepdims=True)
            powers = jnp.exp2((scores - top) * SCALE_LOG2E)
            weight[c, g] = powers
            total = jnp.sum(powers, axis=0, keepdims=True)
            grad_probs = lax.dot_general(
                values, nearby(c, 1, g), contract, preferred_element_type=jnp.float32
            )
            gprob[c, g] = grad_probs
            mixed = jnp.sum(powers * grad_probs, axis=0, keepdims=True)
            for n in range(5):
                span = slice(n * BLOCK, (n + 1) * BLOCK)
                for at, row in enumerate((top, total, mixed)):
                    if n == OWN:
                        st_own[c, 3 * g + at] = row[:, span]
                    else:
                        st_out[n, c, 3 * g + at] = row[:, span]
        for n in (F, X, Y, C):
            guarded(present[n], lambda n=n: st_copy(n, c).start())

    def stage_combine(c):
        for n in (C, Y, X, F):
            guarded(present[n], lambda n=n: st_copy(n, c).wait_recv())
        for g in range(GROUP):
            tops = [st_own[c, 3 * g]] + [st_in[n, c, 3 * g] for n in (C, Y, X, F)]
            totals = [st_own[c, 3 * g + 1]] + [st_in[n, c, 3 * g + 1] for n in (C, Y, X, F)]
            mixes = [st_own[c, 3 * g + 2]] + [st_in[n, c, 3 * g + 2] for n in (C, Y, X, F)]
            top = functools.reduce(jnp.maximum, tops)
            shares = [jnp.exp2((each - top) * SCALE_LOG2E) for each in tops]
            total = sum(share * each for share, each in zip(shares, totals))
            inverse = 1.0 / total
            delta = sum(share * each for share, each in zip(shares, mixes)) * inverse
            fin_own[c, 2 * g] = shares[OWN] * inverse
            fin_own[c, 2 * g + 1] = delta
            for n in (C, Y, X, F):
                fin_out[n, c, 2 * g] = shares[n] * inverse
                fin_out[n, c, 2 * g + 1] = delta
        for n in (F, X, Y, C):
            guarded(present[n], lambda n=n: fin_copy(n, c).start())

    def stage_phase2(c):
        for n in (C, Y, X, F):
            guarded(present[n], lambda n=n: fin_copy(n, c).wait_recv())
        for g in range(GROUP):
            cols = head_cols(c, g)
            factor = jnp.concatenate(
                [fin_own[c, 2 * g]] + [fin_in[n, c, 2 * g] for n in (C, Y, X, F)], axis=1
            )
            delta = jnp.concatenate(
                [fin_own[c, 2 * g + 1]] + [fin_in[n, c, 2 * g + 1] for n in (C, Y, X, F)], axis=1
            )
            powers = weight[c, g]
            probs = powers * factor
            grad_scores = (probs * ((gprob[c, g] - delta) * SCALE)).astype(jnp.bfloat16)
            plain = (((1,), (0,)), ((), ()))
            dv_out[0, 0, :, cols] = lax.dot_general(
                probs.astype(jnp.bfloat16),
                nearby(c, 1, g),
                plain,
                preferred_element_type=jnp.float32,
            ).astype(jnp.bfloat16)
            dk_out[0, 0, :, cols] = lax.dot_general(
                grad_scores, nearby(c, 0, g), plain, preferred_element_type=jnp.float32
            ).astype(jnp.bfloat16)
            turned = lax.dot_general(
                k_ref[:, cols],
                grad_scores,
                (((0,), (0,)), ((), ())),
                preferred_element_type=jnp.float32,
            )
            dq_own[0, c, g] = turned[:, :BLOCK]
            dq_own[1, c, g] = turned[:, X * BLOCK : (X + 1) * BLOCK]
            for n in (C, Y, F):
                dq_send[n, c, g] = turned[:, n * BLOCK : (n + 1) * BLOCK].astype(jnp.bfloat16)
        guarded(has_f, lambda: dq_copy(F, c).start())
        guarded(has_y, lambda: dq_copy(Y, c).start())
        dq_copy(C, c).start()

    def stage_xret(c):
        guarded(has_zout, lambda: dq_copy(F, c).wait_recv())

        @pl.when(bent)
        def _():
            dq_copy(Y, c).wait_recv()
            for g in range(GROUP):
                dq_own[1, c, g] = dq_own[1, c, g] + dq_in[Y, c, g].astype(jnp.float32)
                dq_in[Y, c, g] = jnp.zeros(dq_in.shape[3:], dq_in.dtype)

        for g in range(GROUP):
            dq_send[X, c, g] = (dq_own[1, c, g] + dq_in[F, c, g].astype(jnp.float32)).astype(
                jnp.bfloat16
            )
        dq_copy(X, c).start()

    def stage_final(c):
        dq_copy(C, c).wait_recv()
        guarded(straight, lambda: dq_copy(Y, c).wait_recv())
        dq_copy(X, c).wait_recv()
        for g in range(GROUP):
            total = dq_own[0, c, g]
            for n in (C, Y, X):
                total = total + dq_in[n, c, g].astype(jnp.float32)
            dq_out[0, 0, :, head_cols(c, g)] = total.T.astype(jnp.bfloat16)

    stages = (
        (0, stage_relay),
        (LAG_PHASE1, stage_phase1),
        (LAG_COMBINE, stage_combine),
        (LAG_PHASE2, stage_phase2),
        (LAG_XRET, stage_xret),
        (LAG_FINAL, stage_final),
    )

    @pl.loop(0, chunks + LAG_FINAL)
    def _(tick):
        for lag, stage in stages:

            @pl.when((tick >= lag) & (tick < chunks + lag))
            def _(lag=lag, stage=stage):
                stage(tick - lag)

    for n in (X, F, C, Y):
        guarded(present[n], lambda n=n: bias_copy(n).wait_send())

    @pl.loop(0, chunks)
    def _(c):
        forward(X, c).wait_send()
        forward(C, c).wait_send()
        guarded(has_y, lambda: bent_forward(c).wait_send())
        guarded(has_zout, lambda: relay(c).wait_send())
        for n in (C, Y, X, F):
            guarded(present[n], lambda n=n: st_copy(n, c).wait_send())
            guarded(present[n], lambda n=n: fin_copy(n, c).wait_send())
            guarded(present[n], lambda n=n: dq_copy(n, c).wait_send())


def body(slabs, bands, queries, key_states, value_states, grad_out, window):
    features = queries.shape[3]
    heads = features // HEAD_DIM
    chunks = heads // GROUP
    wide = GROUP * HEAD_DIM
    f32, bf16 = jnp.float32, jnp.bfloat16
    dma = pltpu.SemaphoreType.DMA
    out = jax.ShapeDtypeStruct(queries.shape, bf16)
    anywhere = pl.BlockSpec(memory_space=pl.ANY)
    vmem = pl.BlockSpec(memory_space=pltpu.VMEM)
    macs = heads * 5 * 5 * BLOCK * BLOCK * HEAD_DIM
    return pl.pallas_call(
        functools.partial(kernel, slabs, bands, chunks),
        out_shape=(out, out, out),
        in_specs=[anywhere] * 4 + [pl.BlockSpec(memory_space=pltpu.SMEM)],
        out_specs=(vmem, vmem, vmem),
        scratch_shapes=[
            pltpu.VMEM((BLOCK, features), bf16),
            pltpu.VMEM((BLOCK, features), bf16),
            pltpu.VMEM((5, chunks, 2, BLOCK, wide), bf16),
            pltpu.VMEM((chunks, GROUP, BLOCK, 5 * BLOCK), f32),
            pltpu.VMEM((chunks, GROUP, BLOCK, 5 * BLOCK), f32),
            pltpu.VMEM((5, 2, 1, BLOCK), f32),
            pltpu.VMEM((5, 2, 1, BLOCK), f32),
            pltpu.VMEM((chunks, 3 * GROUP, 1, BLOCK), f32),
            pltpu.VMEM((5, chunks, 3 * GROUP, 1, BLOCK), f32),
            pltpu.VMEM((5, chunks, 3 * GROUP, 1, BLOCK), f32),
            pltpu.VMEM((chunks, 2 * GROUP, 1, BLOCK), f32),
            pltpu.VMEM((5, chunks, 2 * GROUP, 1, BLOCK), f32),
            pltpu.VMEM((5, chunks, 2 * GROUP, 1, BLOCK), f32),
            pltpu.VMEM((2, chunks, GROUP, HEAD_DIM, BLOCK), f32),
            pltpu.VMEM((5, chunks, GROUP, HEAD_DIM, BLOCK), bf16),
            pltpu.VMEM((5, chunks, GROUP, HEAD_DIM, BLOCK), bf16),
            dma((3, chunks)),
            dma((5,)),
            dma((5,)),
            dma((5, chunks)),
            dma((5, chunks)),
            dma((5, chunks)),
            dma((5, chunks)),
            dma((5, chunks)),
            dma((5, chunks)),
            dma((5, chunks)),
            dma((5, chunks)),
        ],
        compiler_params=pltpu.CompilerParams(
            collective_id=0, has_side_effects=True, vmem_limit_bytes=40 << 20
        ),
        cost_estimate=pl.CostEstimate(
            flops=2 * macs,
            bytes_accessed=7 * BLOCK * features * 2,
            transcendentals=heads * 5 * BLOCK * BLOCK,
        ),
    )(queries, key_states, value_states, grad_out, window)


def solution(mesh):
    spec = P("tm", "space", None, None)
    return jax.shard_map(
        functools.partial(body, mesh.shape["tm"], mesh.shape["space"]),
        mesh=mesh,
        in_specs=(spec,) * 5,
        out_specs=(spec,) * 3,
        check_vma=False,
    )
```

```python
import functools
import math

import jax
import jax.numpy as jnp
from jax import lax
from jax.experimental import pallas as pl
from jax.experimental.pallas import tpu as pltpu
from jax.sharding import PartitionSpec as P

MESH = pl.DeviceIdType.MESH
HEAD_DIM = 128
TILE_TOKENS = 64
BLOCK = 128
MASKED = -1e30
SCALE = HEAD_DIM ** (-0.5)
SCALE_LOG2E = SCALE * math.log2(math.e)

OWN, C, Y, X, F = range(5)
RETURNED = 6
AHEAD = 3
LAG_ARRIVED, LAG_COMBINE, LAG_PHASE2, LAG_XRET, LAG_FINAL = 3, 6, 9, 12, 15


def kernel(
    slabs,
    bands,
    heads,
    q_hbm,
    k_hbm,
    v_hbm,
    g_hbm,
    window,
    dq_out,
    dk_out,
    dv_out,
    k_ref,
    v_ref,
    fw,
    weight,
    gprob,
    bias_out,
    bias_in,
    st_own,
    st_out,
    st_in,
    fin_own,
    fin_out,
    fin_in,
    row_own,
    row_in,
    dq_own,
    dq_send,
    dq_in,
    load_sem,
    bias_ssem,
    bias_rsem,
    fwd_ssem,
    fwd_rsem,
    st_ssem,
    st_rsem,
    fin_ssem,
    fin_rsem,
    row_ssem,
    row_rsem,
    dq_ssem,
    dq_rsem,
):
    local = heads - RETURNED
    messages = RETURNED + 2 * local
    t = lax.axis_index("tm")
    b = lax.axis_index("space")
    todd = lax.rem(t, 2)
    bodd = lax.rem(b, 2)
    tstep = 2 * todd - 1
    bstep = 1 - 2 * bodd
    t_c = t - tstep
    t_y = t + tstep
    b_x = b + bstep
    b_f = b - bstep
    b_zout = b + 2 * bstep
    b_zin = b - 2 * bstep
    has_y = (t_y >= 0) & (t_y < slabs)
    has_f = (b_f >= 0) & (b_f < bands)
    has_zout = (b_zout >= 0) & (b_zout < bands)
    bent = (t == slabs // 2 - 1) | (t == slabs // 2)
    straight = has_y & jnp.logical_not(bent)
    b_y = jnp.where(bent, b_x, b)

    partner = {C: (t_c, b), Y: (t_y, b), X: (t, b_x), F: (t, b_f)}
    present = {C: None, Y: has_y, X: None, F: has_f}
    bulk_y = (t_y, b_y)
    zout, zin = (t, b_zout), (t, b_zin)

    def guarded(condition, action):
        if condition is None:
            action()
        else:
            pl.when(condition)(action)

    def head_cols(h):
        return pl.ds(pl.multiple_of(h * HEAD_DIM, HEAD_DIM), HEAD_DIM)

    def load(m, h, src, piece):
        return pltpu.make_async_copy(
            src.at[0, 0, :, head_cols(h)], fw.at[OWN, m, piece], load_sem.at[piece, m]
        )

    def each_load(m, act):
        @pl.when(m < RETURNED)
        def _():
            act(load(m, m, q_hbm, 0))
            act(load(m, m, g_hbm, 1))

        @pl.when((m >= RETURNED) & (m < heads))
        def _():
            act(load(m, m, k_hbm, 0))
            act(load(m, m, v_hbm, 1))

        @pl.when(m >= heads)
        def _():
            act(load(m, m - local, q_hbm, 0))
            act(load(m, m - local, g_hbm, 1))

    k_load = pltpu.make_async_copy(k_hbm.at[0, 0], k_ref, load_sem.at[2, 0])
    v_load = pltpu.make_async_copy(v_hbm.at[0, 0], v_ref, load_sem.at[2, 1])

    @pl.loop(0, messages)
    def _(m):
        each_load(m, lambda copy: copy.start())

    k_load.start()
    v_load.start()

    barrier = pltpu.get_barrier_semaphore()

    def greet(device):
        pl.semaphore_signal(barrier, inc=1, device_id=device, device_id_type=MESH)

    for n in (C, Y, X, F):
        guarded(present[n], functools.partial(greet, partner[n]))
    guarded(bent, functools.partial(greet, bulk_y))
    guarded(has_zout, functools.partial(greet, zout))
    guarded(has_f, functools.partial(greet, zin))

    lane_tile = lax.broadcasted_iota(jnp.int32, (1, BLOCK), 1) // TILE_TOKENS
    dirs = {
        OWN: (0, 0),
        C: (-tstep, 0),
        Y: (tstep, 0),
        X: (0, bstep),
        F: (0, -bstep),
    }
    for n in (OWN, C, Y, X, F):
        dt, dr = dirs[n]
        for key_tile in range(2):
            row = None
            for query_tile in range(2):
                dc = key_tile - query_tile
                if n == OWN and dc == 0:
                    value = jnp.float32(0.0)
                else:
                    code = 9 * (dt + 1) + 3 * (dr + 1) + dc + 1
                    listed = window[0, 0, query_tile, code]
                    shown = listed == 1
                    if n != OWN and present[n] is not None:
                        shown = shown & present[n]
                    value = jnp.where(shown, 0.0, MASKED).astype(jnp.float32)
                part = jnp.full((1, BLOCK), value, jnp.float32)
                row = part if row is None else jnp.where(lane_tile == 0, row, part)
            if n == OWN:
                bias_in[OWN, key_tile] = row
            else:
                bias_out[n, key_tile] = row

    def blank(n):
        bias_in[n] = jnp.zeros_like(bias_in[n])

        @pl.loop(0, messages)
        def _(m):
            fw[n, m] = jnp.zeros(fw.shape[2:], fw.dtype)

        zero_row = jnp.zeros((1, BLOCK), jnp.float32)

        @pl.loop(0, RETURNED)
        def _(h):
            st_in[n, h, 0] = jnp.full((1, BLOCK), MASKED, jnp.float32)
            st_in[n, h, 1] = zero_row
            st_in[n, h, 2] = zero_row
            fin_in[n, h, 0] = zero_row
            fin_in[n, h, 1] = zero_row
            if n != F:
                dq_in[n, h] = jnp.zeros(dq_in.shape[2:], dq_in.dtype)

        @pl.loop(0, local)
        def _(j):
            for at in range(3):
                row_in[n, j, at] = zero_row

    pl.when(jnp.logical_not(has_y))(functools.partial(blank, Y))
    pl.when(jnp.logical_not(has_f))(functools.partial(blank, F))

    @pl.when(jnp.logical_not(has_zout))
    def _():
        @pl.loop(0, RETURNED)
        def _(h):
            dq_in[F, h] = jnp.zeros(dq_in.shape[2:], dq_in.dtype)

    count = 2 + 2 * has_f.astype(jnp.int32) + has_y.astype(jnp.int32)
    count = count + bent.astype(jnp.int32) + has_zout.astype(jnp.int32)
    pl.semaphore_wait(barrier, count)

    def remote(src, dst, send, recv, device):
        return pltpu.make_async_remote_copy(
            src_ref=src,
            dst_ref=dst,
            send_sem=send,
            recv_sem=recv,
            device_id=device,
            device_id_type=MESH,
        )

    def bias_copy(n):
        return remote(
            bias_out.at[n], bias_in.at[n], bias_ssem.at[n], bias_rsem.at[n], partner[n]
        )

    def forward(n, c):
        return remote(
            fw.at[OWN, c], fw.at[n, c], fwd_ssem.at[n, c], fwd_rsem.at[n, c], partner[n]
        )

    def bent_forward(c):
        return remote(fw.at[X, c], fw.at[Y, c], fwd_ssem.at[Y, c], fwd_rsem.at[Y, c], bulk_y)

    def relay(c):
        return remote(fw.at[X, c], fw.at[F, c], fwd_ssem.at[F, c], fwd_rsem.at[F, c], zout)

    def st_copy(n, c):
        return remote(
            st_out.at[n, c], st_in.at[n, c], st_ssem.at[n, c], st_rsem.at[n, c], partner[n]
        )

    def fin_copy(n, c):
        return remote(
            fin_out.at[n, c], fin_in.at[n, c], fin_ssem.at[n, c], fin_rsem.at[n, c], partner[n]
        )

    def row_copy(n, j):
        return remote(
            row_own.at[j], row_in.at[n, j], row_ssem.at[n, j], row_rsem.at[n, j], partner[n]
        )

    def dq_copy(n, c):
        device = {C: partner[C], Y: bulk_y, X: partner[X], F: zin}[n]
        return remote(
            dq_send.at[n, c], dq_in.at[n, c], dq_ssem.at[n, c], dq_rsem.at[n, c], device
        )

    for n in (X, F, C, Y):
        guarded(present[n], lambda n=n: bias_copy(n).start())

    def send_own(m):
        each_load(m, lambda copy: copy.wait())
        forward(X, m).start()
        forward(C, m).start()

        @pl.when(straight)
        def _():
            forward(Y, m).start()

    @pl.loop(0, AHEAD)
    def _(m):
        send_own(m)

    k_load.wait()
    v_load.wait()
    for n in (X, F, C, Y):
        guarded(present[n], lambda n=n: bias_copy(n).wait_recv())

    def nearby(m, piece):
        return jnp.concatenate([fw[n, m, piece] for n in range(5)], axis=0)

    def dot(a, b, a_dim, b_dim):
        return lax.dot_general(
            a, b, (((a_dim,), (b_dim,)), ((), ())), preferred_element_type=jnp.float32
        )

    def masked_for_own_keys(scores):
        masks = [
            jnp.concatenate([bias_in[n, key_tile] for n in range(5)], axis=1)
            for key_tile in range(2)
        ]
        return jnp.concatenate(
            [scores[:TILE_TOKENS] + masks[0], scores[TILE_TOKENS:] + masks[1]], axis=0
        )

    def arrived(m):
        forward(C, m).wait_recv()

        @pl.when(has_y)
        def _():
            forward(Y, m).wait_recv()

        @pl.when(has_f)
        def _():
            relay(m).wait_recv()

    def to_neighbours(copy, at):
        for n in (F, X, Y, C):
            guarded(present[n], lambda n=n: copy(n, at).start())

    def from_neighbours(copy, at):
        for n in (C, Y, X, F):
            guarded(present[n], lambda n=n: copy(n, at).wait_recv())

    def stage_relay(m):
        forward(X, m).wait_recv()

        @pl.when(has_zout)
        def _():
            relay(m).start()

        @pl.when(bent)
        def _():
            bent_forward(m).start()

        @pl.when(m + AHEAD < messages)
        def _():
            send_own(m + AHEAD)

    def stage_phase1(h):
        arrived(h)
        cols = head_cols(h)
        scores = masked_for_own_keys(dot(k_ref[:, cols], nearby(h, 0), 1, 1))
        top = jnp.max(scores, axis=0, keepdims=True)
        powers = jnp.exp2((scores - top) * SCALE_LOG2E)
        weight[h] = powers
        total = jnp.sum(powers, axis=0, keepdims=True)
        grad_probs = dot(v_ref[:, cols], nearby(h, 1), 1, 1)
        gprob[h] = grad_probs
        mixed = jnp.sum(powers * grad_probs, axis=0, keepdims=True)
        for n in range(5):
            span = slice(n * BLOCK, (n + 1) * BLOCK)
            for at, row in enumerate((top, total, mixed)):
                if n == OWN:
                    st_own[h, at] = row[:, span]
                else:
                    st_out[n, h, at] = row[:, span]
        to_neighbours(st_copy, h)

    def stage_combine(h):
        from_neighbours(st_copy, h)
        tops, totals, mixes = (
            [st_own[h, at]] + [st_in[n, h, at] for n in (C, Y, X, F)] for at in range(3)
        )
        top = functools.reduce(jnp.maximum, tops)
        shares = [jnp.exp2((each - top) * SCALE_LOG2E) for each in tops]
        inverse = 1.0 / sum(share * each for share, each in zip(shares, totals))
        delta = sum(share * each for share, each in zip(shares, mixes)) * inverse
        fin_own[h, 0] = shares[OWN] * inverse
        fin_own[h, 1] = delta
        for n in (C, Y, X, F):
            fin_out[n, h, 0] = shares[n] * inverse
            fin_out[n, h, 1] = delta
        to_neighbours(fin_copy, h)

    def own_key_grads(cols, probs, grad_probs, delta, m):
        grad_scores = (probs * ((grad_probs - delta) * SCALE)).astype(jnp.bfloat16)
        dv_out[0, 0, :, cols] = dot(probs.astype(jnp.bfloat16), nearby(m, 1), 1, 0).astype(
            jnp.bfloat16
        )
        dk_out[0, 0, :, cols] = dot(grad_scores, nearby(m, 0), 1, 0).astype(jnp.bfloat16)
        return grad_scores

    def stage_phase2(h):
        from_neighbours(fin_copy, h)
        cols = head_cols(h)
        factor, delta = (
            jnp.concatenate([fin_own[h, at]] + [fin_in[n, h, at] for n in (C, Y, X, F)], axis=1)
            for at in range(2)
        )
        grad_scores = own_key_grads(cols, weight[h] * factor, gprob[h], delta, h)
        turned = dot(k_ref[:, cols], grad_scores, 0, 0)
        dq_own[0, h] = turned[:, :BLOCK]
        dq_own[1, h] = turned[:, X * BLOCK : (X + 1) * BLOCK]
        for n in (C, Y, F):
            dq_send[n, h] = turned[:, n * BLOCK : (n + 1) * BLOCK].astype(jnp.bfloat16)
        guarded(has_f, lambda: dq_copy(F, h).start())
        guarded(has_y, lambda: dq_copy(Y, h).start())
        dq_copy(C, h).start()

    def stage_xret(h):
        guarded(has_zout, lambda: dq_copy(F, h).wait_recv())

        @pl.when(bent)
        def _():
            dq_copy(Y, h).wait_recv()
            dq_own[1, h] = dq_own[1, h] + dq_in[Y, h].astype(jnp.float32)
            dq_in[Y, h] = jnp.zeros(dq_in.shape[2:], dq_in.dtype)

        dq_send[X, h] = (dq_own[1, h] + dq_in[F, h].astype(jnp.float32)).astype(jnp.bfloat16)
        dq_copy(X, h).start()

    def stage_final(h):
        dq_copy(C, h).wait_recv()
        guarded(straight, lambda: dq_copy(Y, h).wait_recv())
        dq_copy(X, h).wait_recv()
        total = dq_own[0, h]
        for n in (C, Y, X):
            total = total + dq_in[n, h].astype(jnp.float32)
        dq_out[0, 0, :, head_cols(h)] = total.T.astype(jnp.bfloat16)

    def stage_own_rows(j):
        kv, qg = RETURNED + j, heads + j
        arrived(kv)
        keys = nearby(kv, 0)
        scores = dot(keys, fw[OWN, qg, 0], 1, 1)
        parts = []
        for n in range(5):
            for key_tile in range(2):
                mask = bias_in[OWN, key_tile] if n == OWN else bias_out[n, key_tile]
                first = n * BLOCK + key_tile * TILE_TOKENS
                parts.append(scores[first : first + TILE_TOKENS] + mask)
        scores = jnp.concatenate(parts, axis=0)
        top = jnp.max(scores, axis=0, keepdims=True)
        powers = jnp.exp2((scores - top) * SCALE_LOG2E)
        inverse = 1.0 / jnp.sum(powers, axis=0, keepdims=True)
        grad_probs = dot(nearby(kv, 1), fw[OWN, qg, 1], 1, 1)
        probs = powers * inverse
        delta = jnp.sum(probs * grad_probs, axis=0, keepdims=True)
        for at, row in enumerate((top, inverse, delta)):
            row_own[j, at] = row
        to_neighbours(row_copy, j)
        grad_scores = (probs * ((grad_probs - delta) * SCALE)).astype(jnp.bfloat16)
        dq_out[0, 0, :, head_cols(RETURNED + j)] = dot(keys, grad_scores, 0, 0).T.astype(
            jnp.bfloat16
        )

    def stage_own_keys(j):
        kv, qg = RETURNED + j, heads + j
        arrived(qg)
        from_neighbours(row_copy, j)
        top, inverse, delta = (
            jnp.concatenate([row_own[j, at]] + [row_in[n, j, at] for n in (C, Y, X, F)], axis=1)
            for at in range(3)
        )
        scores = masked_for_own_keys(dot(fw[OWN, kv, 0], nearby(qg, 0), 1, 1))
        probs = jnp.exp2((scores - top) * SCALE_LOG2E) * inverse
        grad_probs = dot(fw[OWN, kv, 1], nearby(qg, 1), 1, 1)
        own_key_grads(head_cols(RETURNED + j), probs, grad_probs, delta, qg)

    stages = (
        (0, messages, stage_relay),
        (LAG_FINAL, RETURNED, stage_final),
        (LAG_XRET, RETURNED, stage_xret),
        (LAG_PHASE2, RETURNED, stage_phase2),
        (LAG_COMBINE, RETURNED, stage_combine),
        (LAG_ARRIVED, RETURNED, stage_phase1),
        (LAG_ARRIVED + RETURNED, local, stage_own_rows),
        (LAG_ARRIVED + heads, local, stage_own_keys),
    )

    @pl.loop(0, max(messages + LAG_ARRIVED, RETURNED + LAG_FINAL))
    def _(tick):
        for lag, count, stage in stages:

            @pl.when((tick >= lag) & (tick < count + lag))
            def _(lag=lag, stage=stage):
                stage(tick - lag)

    for n in (X, F, C, Y):
        guarded(present[n], lambda n=n: bias_copy(n).wait_send())

    @pl.loop(0, messages)
    def _(m):
        forward(X, m).wait_send()
        forward(C, m).wait_send()
        guarded(has_y, lambda: bent_forward(m).wait_send())
        guarded(has_zout, lambda: relay(m).wait_send())

    for count, copies in ((RETURNED, (st_copy, fin_copy, dq_copy)), (local, (row_copy,))):

        @pl.loop(0, count)
        def _(at, copies=copies):
            for copy in copies:
                for n in (C, Y, X, F):
                    guarded(present[n], lambda n=n, copy=copy: copy(n, at).wait_send())


def store(a, b, c, a_out, b_out, c_out, sems):
    pairs = ((a, a_out), (b, b_out), (c, c_out))
    copies = [pltpu.make_async_copy(x, y, sems.at[i]) for i, (x, y) in enumerate(pairs)]
    for copy in copies:
        copy.start()
    for copy in copies:
        copy.wait()


def body(slabs, bands, queries, key_states, value_states, grad_out, window):
    features = queries.shape[3]
    heads = features // HEAD_DIM
    local = heads - RETURNED
    messages = RETURNED + 2 * local
    f32, bf16 = jnp.float32, jnp.bfloat16
    dma = pltpu.SemaphoreType.DMA
    out = jax.ShapeDtypeStruct(queries.shape, bf16)
    anywhere = pl.BlockSpec(memory_space=pl.ANY)
    vmem = pl.BlockSpec(memory_space=pltpu.VMEM)
    macs = heads * 5 * 5 * BLOCK * BLOCK * HEAD_DIM
    outs = pl.pallas_call(
        functools.partial(kernel, slabs, bands, heads),
        out_shape=(out, out, out),
        in_specs=[anywhere] * 4 + [pl.BlockSpec(memory_space=pltpu.SMEM)],
        out_specs=(vmem, vmem, vmem),
        scratch_shapes=[
            pltpu.VMEM((BLOCK, features), bf16),
            pltpu.VMEM((BLOCK, features), bf16),
            pltpu.VMEM((5, messages, 2, BLOCK, HEAD_DIM), bf16),
            pltpu.VMEM((RETURNED, BLOCK, 5 * BLOCK), f32),
            pltpu.VMEM((RETURNED, BLOCK, 5 * BLOCK), f32),
            pltpu.VMEM((5, 2, 1, BLOCK), f32),
            pltpu.VMEM((5, 2, 1, BLOCK), f32),
            pltpu.VMEM((RETURNED, 3, 1, BLOCK), f32),
            pltpu.VMEM((5, RETURNED, 3, 1, BLOCK), f32),
            pltpu.VMEM((5, RETURNED, 3, 1, BLOCK), f32),
            pltpu.VMEM((RETURNED, 2, 1, BLOCK), f32),
            pltpu.VMEM((5, RETURNED, 2, 1, BLOCK), f32),
            pltpu.VMEM((5, RETURNED, 2, 1, BLOCK), f32),
            pltpu.VMEM((local, 3, 1, BLOCK), f32),
            pltpu.VMEM((5, local, 3, 1, BLOCK), f32),
            pltpu.VMEM((2, RETURNED, HEAD_DIM, BLOCK), f32),
            pltpu.VMEM((5, RETURNED, HEAD_DIM, BLOCK), bf16),
            pltpu.VMEM((5, RETURNED, HEAD_DIM, BLOCK), bf16),
            dma((3, messages)),
            dma((5,)),
            dma((5,)),
            dma((5, messages)),
            dma((5, messages)),
            dma((5, RETURNED)),
            dma((5, RETURNED)),
            dma((5, RETURNED)),
            dma((5, RETURNED)),
            dma((5, local)),
            dma((5, local)),
            dma((5, RETURNED)),
            dma((5, RETURNED)),
        ],
        compiler_params=pltpu.CompilerParams(
            collective_id=0, has_side_effects=True, vmem_limit_bytes=62 << 20
        ),
        cost_estimate=pl.CostEstimate(
            flops=2 * macs,
            bytes_accessed=7 * BLOCK * features * 2,
            transcendentals=heads * 5 * BLOCK * BLOCK,
        ),
    )(queries, key_states, value_states, grad_out, window)

    return pl.pallas_call(
        store,
        out_shape=(out, out, out),
        in_specs=[vmem] * 3,
        out_specs=[anywhere] * 3,
        scratch_shapes=[dma((3,))],
    )(*outs)


def solution(mesh):
    spec = P("tm", "space", None, None)
    return jax.shard_map(
        functools.partial(body, mesh.shape["tm"], mesh.shape["space"]),
        mesh=mesh,
        in_specs=(spec,) * 5,
        out_specs=(spec,) * 3,
        check_vma=False,
    )
```

```python
import functools
import math

import jax
import jax.numpy as jnp
from jax import lax
from jax.experimental import pallas as pl
from jax.experimental.pallas import tpu as pltpu
from jax.sharding import PartitionSpec as P

MESH = pl.DeviceIdType.MESH
HEAD_DIM = 128
TILE_TOKENS = 64
BLOCK = 128
MASKED = -1e30
SCALE = HEAD_DIM ** (-0.5)
SCALE_LOG2E = SCALE * math.log2(math.e)

OWN, C, Y, X, F = range(5)
RETURNED = 6
AHEAD = 3
LAG_ARRIVED, LAG_COMBINE, LAG_PHASE2, LAG_XRET, LAG_FINAL = 3, 6, 9, 12, 15


def kernel(
    slabs,
    bands,
    heads,
    q_hbm,
    k_hbm,
    v_hbm,
    g_hbm,
    window_hbm,
    dq_out,
    dk_out,
    dv_out,
    window,
    k_ref,
    v_ref,
    fw,
    weight,
    gprob,
    bias_out,
    bias_in,
    st_own,
    st_out,
    st_in,
    fin_own,
    fin_out,
    fin_in,
    row_own,
    row_in,
    dq_own,
    dq_send,
    dq_in,
    load_sem,
    bias_ssem,
    bias_rsem,
    fwd_ssem,
    x_rsem,
    arr_rsem,
    st_ssem,
    st_rsem,
    fin_ssem,
    fin_rsem,
    row_ssem,
    row_rsem,
    dq_ssem,
    dq_rsem,
):
    local = heads - RETURNED
    messages = RETURNED + 2 * local
    t = lax.axis_index("tm")
    b = lax.axis_index("space")
    todd = lax.rem(t, 2)
    bodd = lax.rem(b, 2)
    tstep = 2 * todd - 1
    bstep = 1 - 2 * bodd
    t_c = t - tstep
    t_y = t + tstep
    b_x = b + bstep
    b_f = b - bstep
    b_zout = b + 2 * bstep
    b_zin = b - 2 * bstep
    has_y = (t_y >= 0) & (t_y < slabs)
    has_f = (b_f >= 0) & (b_f < bands)
    has_zout = (b_zout >= 0) & (b_zout < bands)
    bent = (t == slabs // 2 - 1) | (t == slabs // 2)
    straight = has_y & jnp.logical_not(bent)
    b_y = jnp.where(bent, b_x, b)

    partner = {C: (t_c, b), Y: (t_y, b), X: (t, b_x), F: (t, b_f)}
    present = {C: None, Y: has_y, X: None, F: has_f}
    bulk_y = (t_y, b_y)
    zout, zin = (t, b_zout), (t, b_zin)

    def guarded(condition, action):
        if condition is None:
            action()
        else:
            pl.when(condition)(action)

    def head_cols(h):
        return pl.ds(pl.multiple_of(h * HEAD_DIM, HEAD_DIM), HEAD_DIM)

    def load(m, h, src, piece):
        return pltpu.make_async_copy(
            src.at[0, 0, :, head_cols(h)],
            fw.at[OWN, m, piece],
            load_sem.at[jnp.where(m < AHEAD, 0, 1)],
        )

    def start_load(m):
        @pl.when(m < RETURNED)
        def _():
            load(m, m, q_hbm, 0).start()
            load(m, m, g_hbm, 1).start()

        @pl.when((m >= RETURNED) & (m < heads))
        def _():
            load(m, m, k_hbm, 0).start()
            load(m, m, v_hbm, 1).start()

        @pl.when(m >= heads)
        def _():
            load(m, m - local, q_hbm, 0).start()
            load(m, m - local, g_hbm, 1).start()

    def wait_load(first, last, sem):
        span = fw.at[OWN, pl.ds(first, last - first)]
        pltpu.make_async_copy(span, span, load_sem.at[sem]).wait()

    k_load = pltpu.make_async_copy(k_hbm.at[0, 0], k_ref, load_sem.at[2])
    v_load = pltpu.make_async_copy(v_hbm.at[0, 0], v_ref, load_sem.at[3])
    window_load = pltpu.make_async_copy(window_hbm, window, load_sem.at[4])

    barrier = pltpu.get_barrier_semaphore()

    def greet(device):
        pl.semaphore_signal(barrier, inc=1, device_id=device, device_id_type=MESH)

    for n in (C, Y, X, F):
        guarded(present[n], functools.partial(greet, partner[n]))
    guarded(bent, functools.partial(greet, bulk_y))
    guarded(has_zout, functools.partial(greet, zout))
    guarded(has_f, functools.partial(greet, zin))

    @pl.loop(0, AHEAD)
    def _(m):
        start_load(m)

    window_load.start()

    count = 2 + 2 * has_f.astype(jnp.int32) + has_y.astype(jnp.int32)
    count = count + bent.astype(jnp.int32) + has_zout.astype(jnp.int32)
    pl.semaphore_wait(barrier, count)

    def remote(src, dst, send, recv, device):
        return pltpu.make_async_remote_copy(
            src_ref=src,
            dst_ref=dst,
            send_sem=send,
            recv_sem=recv,
            device_id=device,
            device_id_type=MESH,
        )

    def bias_copy(n):
        return remote(bias_out.at[n], bias_in.at[n], bias_ssem.at[n], bias_rsem.at[0], partner[n])

    def forward(n, m):
        recv = x_rsem if n == X else arr_rsem
        return remote(fw.at[OWN, m], fw.at[n, m], fwd_ssem.at[n], recv.at[m], partner[n])

    def bent_forward(m):
        return remote(fw.at[X, m], fw.at[Y, m], fwd_ssem.at[Y], arr_rsem.at[m], bulk_y)

    def relay(m):
        return remote(fw.at[X, m], fw.at[F, m], fwd_ssem.at[F], arr_rsem.at[m], zout)

    def st_copy(n, h):
        return remote(st_out.at[n, h], st_in.at[n, h], st_ssem.at[n], st_rsem.at[h], partner[n])

    def fin_copy(n, h):
        return remote(
            fin_out.at[n, h], fin_in.at[n, h], fin_ssem.at[n], fin_rsem.at[h], partner[n]
        )

    def row_copy(n, j):
        return remote(row_own.at[j], row_in.at[n, j], row_ssem.at[n], row_rsem.at[j], partner[n])

    def dq_copy(n, h):
        device = {C: partner[C], Y: bulk_y, X: partner[X], F: zin}[n]
        whose = {C: 0, Y: jnp.where(bent, 1, 0), X: 0, F: 1}[n]
        return remote(
            dq_send.at[n, h], dq_in.at[n, h], dq_ssem.at[n], dq_rsem.at[whose, h], device
        )

    def landed(span, sem):
        remote(span, span, fwd_ssem.at[OWN], sem, partner[C]).wait_recv()

    def sent(span, sem):
        remote(span, span, sem, x_rsem.at[0], partner[C]).wait_send()

    def by_count(least, act):
        for more, condition in (
            (2, has_y & has_f),
            (1, has_y != has_f),
            (0, jnp.logical_not(has_y | has_f)),
        ):
            pl.when(condition)(functools.partial(act, least + more))

    def send_own(m):
        forward(X, m).start()
        forward(C, m).start()

        @pl.when(straight)
        def _():
            forward(Y, m).start()

    wait_load(0, AHEAD, 0)

    @pl.loop(0, AHEAD)
    def _(m):
        send_own(m)

    @pl.loop(AHEAD, messages)
    def _(m):
        start_load(m)

    k_load.start()
    v_load.start()

    window_load.wait()

    lane_tile = lax.broadcasted_iota(jnp.int32, (1, BLOCK), 1) // TILE_TOKENS
    dirs = {
        OWN: (0, 0),
        C: (-tstep, 0),
        Y: (tstep, 0),
        X: (0, bstep),
        F: (0, -bstep),
    }
    for n in (OWN, C, Y, X, F):
        dt, dr = dirs[n]
        for key_tile in range(2):
            row = None
            for query_tile in range(2):
                dc = key_tile - query_tile
                if n == OWN and dc == 0:
                    value = jnp.float32(0.0)
                else:
                    code = 9 * (dt + 1) + 3 * (dr + 1) + dc + 1
                    listed = window[0, 0, query_tile, code]
                    shown = listed == 1
                    if n != OWN and present[n] is not None:
                        shown = shown & present[n]
                    value = jnp.where(shown, 0.0, MASKED).astype(jnp.float32)
                part = jnp.full((1, BLOCK), value, jnp.float32)
                row = part if row is None else jnp.where(lane_tile == 0, row, part)
            if n == OWN:
                bias_in[OWN, key_tile] = row
            else:
                bias_out[n, key_tile] = row

    for n in (X, F, C, Y):
        guarded(present[n], lambda n=n: bias_copy(n).start())

    def blank(n):
        bias_in[n] = jnp.zeros_like(bias_in[n])

        @pl.loop(0, messages)
        def _(m):
            fw[n, m] = jnp.zeros(fw.shape[2:], fw.dtype)

        zero_row = jnp.zeros((1, BLOCK), jnp.float32)

        @pl.loop(0, RETURNED)
        def _(h):
            st_in[n, h, 0] = jnp.full((1, BLOCK), MASKED, jnp.float32)
            st_in[n, h, 1] = zero_row
            st_in[n, h, 2] = zero_row
            fin_in[n, h, 0] = zero_row
            fin_in[n, h, 1] = zero_row
            if n != F:
                dq_in[n, h] = jnp.zeros(dq_in.shape[2:], dq_in.dtype)

        @pl.loop(0, local)
        def _(j):
            for at in range(3):
                row_in[n, j, at] = zero_row

    pl.when(jnp.logical_not(has_y))(functools.partial(blank, Y))
    pl.when(jnp.logical_not(has_f))(functools.partial(blank, F))

    @pl.when(jnp.logical_not(has_zout))
    def _():
        @pl.loop(0, RETURNED)
        def _(h):
            dq_in[F, h] = jnp.zeros(dq_in.shape[2:], dq_in.dtype)

    def nearby(m, piece):
        return jnp.concatenate([fw[n, m, piece] for n in range(5)], axis=0)

    def dot(a, b, a_dim, b_dim):
        return lax.dot_general(
            a, b, (((a_dim,), (b_dim,)), ((), ())), preferred_element_type=jnp.float32
        )

    def masked_for_own_keys(scores):
        masks = [
            jnp.concatenate([bias_in[n, key_tile] for n in range(5)], axis=1)
            for key_tile in range(2)
        ]
        return jnp.concatenate(
            [scores[:TILE_TOKENS] + masks[0], scores[TILE_TOKENS:] + masks[1]], axis=0
        )

    def arrived(m):
        by_count(1, lambda count: landed(fw.at[pl.ds(1, count), m], arr_rsem.at[m]))

    def to_neighbours(copy, at):
        for n in (F, X, Y, C):
            guarded(present[n], lambda n=n: copy(n, at).start())

    def from_neighbours(buffer, at, sem):
        by_count(2, lambda count: landed(buffer.at[pl.ds(1, count), at], sem.at[at]))

    def stage_relay(m):
        forward(X, m).wait_recv()

        @pl.when(has_zout)
        def _():
            relay(m).start()

        @pl.when(bent)
        def _():
            bent_forward(m).start()

        @pl.when(m + AHEAD < messages)
        def _():
            send_own(m + AHEAD)

    def stage_phase1(h):
        arrived(h)
        cols = head_cols(h)
        scores = masked_for_own_keys(dot(k_ref[:, cols], nearby(h, 0), 1, 1))
        top = jnp.max(scores, axis=0, keepdims=True)
        powers = jnp.exp2((scores - top) * SCALE_LOG2E)
        weight[h] = powers
        total = jnp.sum(powers, axis=0, keepdims=True)
        grad_probs = dot(v_ref[:, cols], nearby(h, 1), 1, 1)
        gprob[h] = grad_probs
        mixed = jnp.sum(powers * grad_probs, axis=0, keepdims=True)
        for n in range(5):
            span = slice(n * BLOCK, (n + 1) * BLOCK)
            for at, row in enumerate((top, total, mixed)):
                if n == OWN:
                    st_own[h, at] = row[:, span]
                else:
                    st_out[n, h, at] = row[:, span]
        to_neighbours(st_copy, h)

    def stage_combine(h):
        from_neighbours(st_in, h, st_rsem)
        tops, totals, mixes = (
            [st_own[h, at]] + [st_in[n, h, at] for n in (C, Y, X, F)] for at in range(3)
        )
        top = functools.reduce(jnp.maximum, tops)
        shares = [jnp.exp2((each - top) * SCALE_LOG2E) for each in tops]
        inverse = 1.0 / sum(share * each for share, each in zip(shares, totals))
        delta = sum(share * each for share, each in zip(shares, mixes)) * inverse
        fin_own[h, 0] = shares[OWN] * inverse
        fin_own[h, 1] = delta
        for n in (C, Y, X, F):
            fin_out[n, h, 0] = shares[n] * inverse
            fin_out[n, h, 1] = delta
        to_neighbours(fin_copy, h)

    def own_key_grads(cols, probs, grad_probs, delta, m):
        grad_scores = (probs * ((grad_probs - delta) * SCALE)).astype(jnp.bfloat16)
        dv_out[0, 0, :, cols] = dot(probs.astype(jnp.bfloat16), nearby(m, 1), 1, 0).astype(
            jnp.bfloat16
        )
        dk_out[0, 0, :, cols] = dot(grad_scores, nearby(m, 0), 1, 0).astype(jnp.bfloat16)
        return grad_scores

    def stage_phase2(h):
        from_neighbours(fin_in, h, fin_rsem)
        cols = head_cols(h)
        factor, delta = (
            jnp.concatenate([fin_own[h, at]] + [fin_in[n, h, at] for n in (C, Y, X, F)], axis=1)
            for at in range(2)
        )
        grad_scores = own_key_grads(cols, weight[h] * factor, gprob[h], delta, h)
        turned = dot(k_ref[:, cols], grad_scores, 0, 0)
        dq_own[0, h] = turned[:, :BLOCK]
        dq_own[1, h] = turned[:, X * BLOCK : (X + 1) * BLOCK]
        for n in (C, Y, F):
            dq_send[n, h] = turned[:, n * BLOCK : (n + 1) * BLOCK].astype(jnp.bfloat16)
        guarded(has_f, lambda: dq_copy(F, h).start())
        guarded(has_y, lambda: dq_copy(Y, h).start())
        dq_copy(C, h).start()

    def stage_xret(h):
        @pl.when(has_zout & bent)
        def _():
            landed(dq_in.at[pl.ds(1, 2), h], dq_rsem.at[1, h])

        @pl.when(has_zout != bent)
        def _():
            landed(dq_in.at[pl.ds(1, 1), h], dq_rsem.at[1, h])

        @pl.when(bent)
        def _():
            dq_own[1, h] = dq_own[1, h] + dq_in[Y, h].astype(jnp.float32)
            dq_in[Y, h] = jnp.zeros(dq_in.shape[2:], dq_in.dtype)

        dq_send[X, h] = (dq_own[1, h] + dq_in[F, h].astype(jnp.float32)).astype(jnp.bfloat16)
        dq_copy(X, h).start()

    def stage_final(h):
        @pl.when(straight)
        def _():
            landed(dq_in.at[pl.ds(1, 3), h], dq_rsem.at[0, h])

        @pl.when(jnp.logical_not(straight))
        def _():
            landed(dq_in.at[pl.ds(1, 2), h], dq_rsem.at[0, h])

        total = dq_own[0, h]
        for n in (C, Y, X):
            total = total + dq_in[n, h].astype(jnp.float32)
        dq_out[0, 0, :, head_cols(h)] = total.T.astype(jnp.bfloat16)

    def stage_own_rows(j):
        kv, qg = RETURNED + j, heads + j
        arrived(kv)
        keys = nearby(kv, 0)
        scores = dot(keys, fw[OWN, qg, 0], 1, 1)
        parts = []
        for n in range(5):
            for key_tile in range(2):
                mask = bias_in[OWN, key_tile] if n == OWN else bias_out[n, key_tile]
                first = n * BLOCK + key_tile * TILE_TOKENS
                parts.append(scores[first : first + TILE_TOKENS] + mask)
        scores = jnp.concatenate(parts, axis=0)
        top = jnp.max(scores, axis=0, keepdims=True)
        powers = jnp.exp2((scores - top) * SCALE_LOG2E)
        inverse = 1.0 / jnp.sum(powers, axis=0, keepdims=True)
        grad_probs = dot(nearby(kv, 1), fw[OWN, qg, 1], 1, 1)
        probs = powers * inverse
        delta = jnp.sum(probs * grad_probs, axis=0, keepdims=True)
        for at, row in enumerate((top, inverse, delta)):
            row_own[j, at] = row
        to_neighbours(row_copy, j)
        grad_scores = (probs * ((grad_probs - delta) * SCALE)).astype(jnp.bfloat16)
        dq_out[0, 0, :, head_cols(RETURNED + j)] = dot(keys, grad_scores, 0, 0).T.astype(
            jnp.bfloat16
        )

    def stage_own_keys(j):
        kv, qg = RETURNED + j, heads + j
        arrived(qg)
        from_neighbours(row_in, j, row_rsem)
        top, inverse, delta = (
            jnp.concatenate([row_own[j, at]] + [row_in[n, j, at] for n in (C, Y, X, F)], axis=1)
            for at in range(3)
        )
        scores = masked_for_own_keys(dot(fw[OWN, kv, 0], nearby(qg, 0), 1, 1))
        probs = jnp.exp2((scores - top) * SCALE_LOG2E) * inverse
        grad_probs = dot(fw[OWN, kv, 1], nearby(qg, 1), 1, 1)
        own_key_grads(head_cols(RETURNED + j), probs, grad_probs, delta, qg)

    stages = (
        (0, messages, stage_relay),
        (LAG_FINAL, RETURNED, stage_final),
        (LAG_XRET, RETURNED, stage_xret),
        (LAG_PHASE2, RETURNED, stage_phase2),
        (LAG_COMBINE, RETURNED, stage_combine),
        (LAG_ARRIVED, RETURNED, stage_phase1),
        (LAG_ARRIVED + RETURNED, local, stage_own_rows),
        (LAG_ARRIVED + heads, local, stage_own_keys),
    )

    wait_load(AHEAD, messages, 1)

    @pl.loop(0, max(messages + LAG_ARRIVED, RETURNED + LAG_FINAL))
    def _(tick):
        @pl.when(tick == LAG_ARRIVED)
        def _():
            k_load.wait()
            v_load.wait()
            by_count(2, lambda count: landed(bias_in.at[pl.ds(1, count)], bias_rsem.at[0]))

        for lag, count, stage in stages:

            @pl.when((tick >= lag) & (tick < count + lag))
            def _(lag=lag, stage=stage):
                stage(tick - lag)

    for n, condition in ((X, None), (C, None), (Y, has_y), (F, has_zout)):
        guarded(condition, lambda n=n: sent(fw.at[OWN], fwd_ssem.at[n]))

    def wait_sends(n):
        sent(bias_out.at[n], bias_ssem.at[n])
        sent(st_out.at[n], st_ssem.at[n])
        sent(fin_out.at[n], fin_ssem.at[n])
        sent(row_own, row_ssem.at[n])
        sent(dq_send.at[n], dq_ssem.at[n])

    for n in (C, Y, X, F):
        guarded(present[n], functools.partial(wait_sends, n))


def store(a, b, c, a_out, b_out, c_out, sems):
    pairs = ((a, a_out), (b, b_out), (c, c_out))
    copies = [pltpu.make_async_copy(x, y, sems.at[i]) for i, (x, y) in enumerate(pairs)]
    for copy in copies:
        copy.start()
    for copy in copies:
        copy.wait()


def body(slabs, bands, queries, key_states, value_states, grad_out, window):
    features = queries.shape[3]
    heads = features // HEAD_DIM
    local = heads - RETURNED
    messages = RETURNED + 2 * local
    f32, bf16 = jnp.float32, jnp.bfloat16
    dma = pltpu.SemaphoreType.DMA
    out = jax.ShapeDtypeStruct(queries.shape, bf16)
    anywhere = pl.BlockSpec(memory_space=pl.ANY)
    vmem = pl.BlockSpec(memory_space=pltpu.VMEM)
    macs = heads * 5 * 5 * BLOCK * BLOCK * HEAD_DIM
    outs = pl.pallas_call(
        functools.partial(kernel, slabs, bands, heads),
        out_shape=(pltpu.VMEM(queries.shape, bf16),) * 3,
        in_specs=[anywhere] * 5,
        out_specs=(vmem, vmem, vmem),
        scratch_shapes=[
            pltpu.SMEM(window.shape, jnp.int32),
            pltpu.VMEM((BLOCK, features), bf16),
            pltpu.VMEM((BLOCK, features), bf16),
            pltpu.VMEM((5, messages, 2, BLOCK, HEAD_DIM), bf16),
            pltpu.VMEM((RETURNED, BLOCK, 5 * BLOCK), f32),
            pltpu.VMEM((RETURNED, BLOCK, 5 * BLOCK), f32),
            pltpu.VMEM((5, 2, 1, BLOCK), f32),
            pltpu.VMEM((5, 2, 1, BLOCK), f32),
            pltpu.VMEM((RETURNED, 3, 1, BLOCK), f32),
            pltpu.VMEM((5, RETURNED, 3, 1, BLOCK), f32),
            pltpu.VMEM((5, RETURNED, 3, 1, BLOCK), f32),
            pltpu.VMEM((RETURNED, 2, 1, BLOCK), f32),
            pltpu.VMEM((5, RETURNED, 2, 1, BLOCK), f32),
            pltpu.VMEM((5, RETURNED, 2, 1, BLOCK), f32),
            pltpu.VMEM((local, 3, 1, BLOCK), f32),
            pltpu.VMEM((5, local, 3, 1, BLOCK), f32),
            pltpu.VMEM((2, RETURNED, HEAD_DIM, BLOCK), f32),
            pltpu.VMEM((5, RETURNED, HEAD_DIM, BLOCK), bf16),
            pltpu.VMEM((5, RETURNED, HEAD_DIM, BLOCK), bf16),
            dma((5,)),
            dma((5,)),
            dma((1,)),
            dma((5,)),
            dma((messages,)),
            dma((messages,)),
            dma((5,)),
            dma((RETURNED,)),
            dma((5,)),
            dma((RETURNED,)),
            dma((5,)),
            dma((local,)),
            dma((5,)),
            dma((2, RETURNED)),
        ],
        compiler_params=pltpu.CompilerParams(
            collective_id=0, has_side_effects=True, vmem_limit_bytes=58 << 20
        ),
        cost_estimate=pl.CostEstimate(
            flops=2 * macs,
            bytes_accessed=7 * BLOCK * features * 2,
            transcendentals=heads * 5 * BLOCK * BLOCK,
        ),
    )(queries, key_states, value_states, grad_out, window)

    return pl.pallas_call(
        store,
        out_shape=(out, out, out),
        in_specs=[vmem] * 3,
        out_specs=[anywhere] * 3,
        scratch_shapes=[dma((3,))],
        compiler_params=pltpu.CompilerParams(vmem_limit_bytes=8 << 20),
    )(*outs)


def solution(mesh):
    spec = P("tm", "space", None, None)
    return jax.shard_map(
        functools.partial(body, mesh.shape["tm"], mesh.shape["space"]),
        mesh=mesh,
        in_specs=(spec,) * 5,
        out_specs=(spec,) * 3,
        check_vma=False,
    )
```

```python
import functools
import math

import jax
import jax.numpy as jnp
from jax import lax
from jax.experimental import pallas as pl
from jax.experimental.pallas import tpu as pltpu
from jax.sharding import PartitionSpec as P

MESH = pl.DeviceIdType.MESH
HEAD_DIM = 128
TILE_TOKENS = 64
BLOCK = 128
MASKED = -1e30
SCALE = HEAD_DIM ** (-0.5)
SCALE_LOG2E = SCALE * math.log2(math.e)

OWN, C, Y, X, F = range(5)
G, H = 1, 2
PAIRS = (OWN, C, X, Y, F)
AHEAD = 3
LAG_SCORES, LAG_COMBINE, LAG_GRADS, LAG_RETURN, LAG_FINAL = 1, 3, 5, 8, 12


def kernel(
    slabs,
    bands,
    heads,
    q_hbm,
    k_hbm,
    v_hbm,
    g_hbm,
    window_hbm,
    dq_out,
    dk_out,
    dv_out,
    window,
    fw,
    kv,
    weight,
    gprob,
    tops,
    bias_out,
    bias_in,
    bias_x,
    st_own,
    st_out,
    st_in,
    fin_own,
    fin_in,
    dq_own,
    dq_send,
    dq_in,
    dkv_own,
    dkv_send,
    dkv_in,
    load_sem,
    bias_ssem,
    bias_rsem,
    fwd_ssem,
    x_rsem,
    arr_rsem,
    st_ssem,
    st_rsem,
    fin_ssem,
    fin_rsem,
    dq_ssem,
    dq_rsem,
    dkv_ssem,
    dkv_rsem,
):
    t = lax.axis_index("tm")
    b = lax.axis_index("space")
    tstep = 2 * lax.rem(t, 2) - 1
    bstep = 1 - 2 * lax.rem(b, 2)
    t_c, t_y = t - tstep, t + tstep
    b_x, b_f = b + bstep, b - bstep
    b_zout, b_zin = b + 2 * bstep, b - 2 * bstep
    has_y = (t_y >= 0) & (t_y < slabs)
    has_f = (b_f >= 0) & (b_f < bands)
    has_zout = (b_zout >= 0) & (b_zout < bands)
    bent = (t == slabs // 2 - 1) | (t == slabs // 2)
    straight = has_y & jnp.logical_not(bent)

    partner = {C: (t_c, b), Y: (t_y, b), X: (t, b_x)}
    reached = {C: None, Y: straight, X: None}
    across, zout, zin = (t_y, b_x), (t, b_zout), (t, b_zin)

    def guarded(condition, action):
        if condition is None:
            action()
        else:
            pl.when(condition)(action)

    def cols(h):
        return pl.ds(pl.multiple_of(h * HEAD_DIM, HEAD_DIM), HEAD_DIM)

    def start_load(h):
        sem = load_sem.at[jnp.where(h < AHEAD, 0, 1)]
        for src, dst in (
            (q_hbm, fw.at[OWN, h, 0]),
            (g_hbm, fw.at[OWN, h, 1]),
            (k_hbm, kv.at[OWN, h, 0]),
            (v_hbm, kv.at[OWN, h, 1]),
        ):
            pltpu.make_async_copy(src.at[0, 0, :, cols(h)], dst, sem).start()

    def wait_load(first, last, sem):
        span = pl.ds(first, last - first)
        both = fw.at[pl.ds(0, 2), span]
        pltpu.make_async_copy(both, both, load_sem.at[sem]).wait()

    window_load = pltpu.make_async_copy(window_hbm, window, load_sem.at[2])

    barrier = pltpu.get_barrier_semaphore()

    def greet(device):
        pl.semaphore_signal(barrier, inc=1, device_id=device, device_id_type=MESH)

    for device, condition in (
        (partner[X], None),
        (partner[C], None),
        (partner[Y], straight),
        (across, bent),
        (zout, has_zout),
        (zin, has_f),
    ):
        guarded(condition, functools.partial(greet, device))

    @pl.loop(0, AHEAD)
    def _(h):
        start_load(h)

    window_load.start()
    count = 2 + has_y.astype(jnp.int32) + has_f.astype(jnp.int32) + has_zout.astype(jnp.int32)
    pl.semaphore_wait(barrier, count)

    def remote(src, dst, send, recv, device):
        return pltpu.make_async_remote_copy(
            src_ref=src,
            dst_ref=dst,
            send_sem=send,
            recv_sem=recv,
            device_id=device,
            device_id_type=MESH,
        )

    def bias_copy(n):
        if n == X:
            return remote(bias_out, bias_x, bias_ssem.at[X], bias_rsem.at[1], partner[X])
        return remote(bias_out.at[n], bias_in.at[n], bias_ssem.at[n], bias_rsem.at[0], partner[n])

    def send_x(h, piece):
        remote(
            fw.at[OWN, h, piece],
            fw.at[X, h, piece],
            fwd_ssem.at[X],
            x_rsem.at[h],
            partner[X],
        ).start()

    def send_own(h):
        send_x(h, 0)
        recv = arr_rsem.at[h]

        @pl.when(has_f)
        def _():
            remote(kv.at[OWN, h], kv.at[G, h], fwd_ssem.at[F], recv, zin).start()

        @pl.when(bent)
        def _():
            remote(kv.at[OWN, h], kv.at[H, h], fwd_ssem.at[Y], recv, across).start()

        @pl.when(straight)
        def _():
            remote(fw.at[OWN, h], fw.at[Y, h], fwd_ssem.at[Y], recv, partner[Y]).start()

        remote(fw.at[OWN, h], fw.at[C, h], fwd_ssem.at[C], recv, partner[C]).start()

    def send_st(n, h):
        remote(
            st_out.at[n, h], st_in.at[n, h], st_ssem.at[n], st_rsem.at[h], partner[n]
        ).start()

    def send_fin(n, h):
        remote(fin_own.at[h], fin_in.at[n, h], fin_ssem.at[n], fin_rsem.at[h], partner[n]).start()

    def send_dq(n, h):
        remote(
            dq_send.at[n, h], dq_in.at[n, h], dq_ssem.at[n], dq_rsem.at[h], partner[n]
        ).start()

    def send_dkv(at, h, device):
        remote(
            dkv_send.at[at, h], dkv_in.at[at, h], dkv_ssem.at[at], dkv_rsem.at[h], device
        ).start()

    def landed(span, sem):
        remote(span, span, fwd_ssem.at[OWN], sem, partner[C]).wait_recv()

    def sent(span, sem):
        remote(span, span, sem, x_rsem.at[0], partner[C]).wait_send()

    def by_count(least, first, second, act):
        for more, condition in (
            (2, first & second),
            (1, first != second),
            (0, jnp.logical_not(first | second)),
        ):
            if least + more:
                pl.when(condition)(functools.partial(act, least + more))

    def from_reached(buffer, h, sem):
        @pl.when(straight)
        def _():
            landed(buffer.at[pl.ds(1, 3), h], sem.at[h])

        @pl.when(jnp.logical_not(straight))
        def _():
            landed(buffer.at[pl.ds(1, 2), h], sem.at[h])

    def to_reached(send, h):
        for n in (X, Y, C):
            guarded(reached[n], functools.partial(send, n, h))

    wait_load(0, AHEAD, 0)

    @pl.loop(0, AHEAD)
    def _(h):
        send_own(h)
        send_x(h, 1)

    @pl.loop(AHEAD, heads)
    def _(h):
        start_load(h)

    window_load.wait()

    lane_tile = lax.broadcasted_iota(jnp.int32, (1, BLOCK), 1) // TILE_TOKENS
    present = {Y: has_y, F: has_f}
    dirs = {
        OWN: (0, 0),
        C: (-tstep, 0),
        Y: (tstep, 0),
        X: (0, bstep),
        F: (0, -bstep),
    }
    for n in (OWN, C, Y, X, F):
        dt, dr = dirs[n]
        for key_tile in range(2):
            row = None
            for query_tile in range(2):
                dc = key_tile - query_tile
                if n == OWN and dc == 0:
                    value = jnp.float32(0.0)
                else:
                    code = 9 * (dt + 1) + 3 * (dr + 1) + dc + 1
                    listed = window[0, 0, query_tile, code]
                    shown = listed == 1
                    if n in present:
                        shown = shown & present[n]
                    value = jnp.where(shown, 0.0, MASKED).astype(jnp.float32)
                part = jnp.full((1, BLOCK), value, jnp.float32)
                row = part if row is None else jnp.where(lane_tile == 0, row, part)
            bias_out[n, key_tile] = row

    for n in (X, C, Y):
        guarded(reached[n], lambda n=n: bias_copy(n).start())

    zero_row = jnp.zeros((1, BLOCK), jnp.float32)

    @pl.when(jnp.logical_not(straight))
    def _():
        bias_in[Y] = jnp.zeros_like(bias_in[Y])

        @pl.loop(0, heads)
        def _(h):
            fw[Y, h] = jnp.zeros(fw.shape[2:], fw.dtype)
            st_in[Y, h, 0] = jnp.full((1, BLOCK), MASKED, jnp.float32)
            for at in (1, 2):
                st_in[Y, h, at] = zero_row
            for at in range(3):
                fin_in[Y, h, at] = zero_row
            dq_in[Y, h] = jnp.zeros(dq_in.shape[2:], dq_in.dtype)

    @pl.when(jnp.logical_not(has_zout))
    def _():
        @pl.loop(0, heads)
        def _(h):
            kv[G, h] = jnp.zeros(kv.shape[2:], kv.dtype)

    for at, condition in ((0, has_f), (1, bent)):

        @pl.when(jnp.logical_not(condition))
        def _(at=at):
            @pl.loop(0, heads)
            def _(h):
                dkv_in[at, h] = jnp.zeros(dkv_in.shape[2:], dkv_in.dtype)

    y_queries = jnp.where(bent, X, Y)
    y_keys = jnp.where(bent, H, OWN)

    def dot(a, b, a_dim, b_dim):
        return lax.dot_general(
            a, b, (((a_dim,), (b_dim,)), ((), ())), preferred_element_type=jnp.float32
        )

    def thrice(h, piece):
        return jnp.concatenate([fw[n, h, piece] for n in (OWN, C, X)], axis=0)

    def products(h, piece):
        return jnp.concatenate(
            [
                dot(kv[OWN, h, piece], thrice(h, piece), 1, 1),
                dot(kv[y_keys, h, piece], fw[y_queries, h, piece], 1, 1),
                dot(kv[G, h, piece], fw[X, h, piece], 1, 1),
            ],
            axis=1,
        )

    def split(row):
        return {n: row[:, i * BLOCK : (i + 1) * BLOCK] for i, n in enumerate(PAIRS)}

    def merged(parts):
        top = functools.reduce(jnp.maximum, [part[0] for part in parts])
        shares = [jnp.exp2((part[0] - top) * SCALE_LOG2E) for part in parts]
        total, mixed = (
            sum(share * part[at] for share, part in zip(shares, parts)) for at in (1, 2)
        )
        return top, total, mixed

    def stage_scores(h):
        by_count(1, has_y, has_zout, lambda count: landed(fw.at[pl.ds(0, count), h], arr_rsem.at[h]))
        masks = []
        for key_tile in range(2):
            y_mask = jnp.where(bent, bias_x[Y, key_tile], bias_in[Y, key_tile])
            rows = [bias_out[OWN, key_tile], bias_in[C, key_tile], bias_x[X, key_tile]]
            masks.append(jnp.concatenate(rows + [y_mask, bias_x[F, key_tile]], axis=1))
        scores = products(h, 0)
        scores = jnp.concatenate(
            [scores[:TILE_TOKENS] + masks[0], scores[TILE_TOKENS:] + masks[1]], axis=0
        )
        top = jnp.max(scores, axis=0, keepdims=True)
        powers = jnp.exp2((scores - top) * SCALE_LOG2E)
        weight[h] = powers
        total = jnp.sum(powers, axis=0, keepdims=True)
        grad_probs = products(h, 1)
        gprob[h] = grad_probs
        mixed = jnp.sum(powers * grad_probs, axis=0, keepdims=True)
        top, total, mixed = split(top), split(total), split(mixed)
        for i, n in enumerate(PAIRS):
            tops[h, i] = top[n]
        part = {n: (top[n], total[n], mixed[n]) for n in PAIRS}
        y_part = (jnp.where(bent, top[Y], MASKED),) + tuple(
            jnp.where(bent, row[Y], 0.0) for row in (total, mixed)
        )
        x_part = merged([part[X], part[F], y_part])
        for at in range(3):
            st_own[h, at] = part[OWN][at]
            st_out[C, h, at] = part[C][at]
            st_out[Y, h, at] = part[Y][at]
            st_out[X, h, at] = x_part[at]
        to_reached(send_st, h)

    def stage_combine(h):
        from_reached(st_in, h, st_rsem)
        parts = [tuple(st_own[h, at] for at in range(3))]
        parts += [tuple(st_in[n, h, at] for at in range(3)) for n in (C, Y, X)]
        top, total, mixed = merged(parts)
        inverse = 1.0 / total
        for at, row in enumerate((top, inverse, mixed * inverse)):
            fin_own[h, at] = row
        to_reached(send_fin, h)

    def stage_grads(h):
        from_reached(fin_in, h, fin_rsem)
        top, inverse, delta = (
            jnp.concatenate(
                [
                    fin_own[h, at],
                    fin_in[C, h, at],
                    fin_in[X, h, at],
                    jnp.where(bent, fin_in[X, h, at], fin_in[Y, h, at]),
                    fin_in[X, h, at],
                ],
                axis=1,
            )
            for at in range(3)
        )
        own_top = jnp.concatenate([tops[h, i] for i in range(5)], axis=1)
        factor = jnp.exp2((own_top - top) * SCALE_LOG2E) * inverse
        probs = weight[h] * factor
        grad_scores = (probs * ((gprob[h] - delta) * SCALE)).astype(jnp.bfloat16)
        probs = probs.astype(jnp.bfloat16)
        third, fourth = 3 * BLOCK, 4 * BLOCK
        own_scores = grad_scores[:, :third]
        y_scores = grad_scores[:, third:fourth]
        g_scores = grad_scores[:, fourth:]
        turned = dot(kv[OWN, h, 0], own_scores, 0, 0)
        y_turned = dot(kv[y_keys, h, 0], y_scores, 0, 0)
        g_turned = dot(kv[G, h, 0], g_scores, 0, 0)
        dq_own[h] = turned[:, :BLOCK]
        dq_send[C, h] = turned[:, BLOCK : 2 * BLOCK].astype(jnp.bfloat16)
        dq_send[Y, h] = y_turned.astype(jnp.bfloat16)
        x_turned = turned[:, 2 * BLOCK :] + g_turned + jnp.where(bent, y_turned, 0.0)
        dq_send[X, h] = x_turned.astype(jnp.bfloat16)
        guarded(straight, lambda: send_dq(Y, h))
        send_dq(C, h)
        for piece, left in enumerate((grad_scores, probs)):
            own = dot(left[:, :third], thrice(h, piece), 1, 0)
            from_y = dot(left[:, third:fourth], fw[y_queries, h, piece], 1, 0)
            from_g = dot(left[:, fourth:], fw[X, h, piece], 1, 0)
            dkv_own[h, piece] = own + jnp.where(bent, 0.0, from_y)
            dkv_send[0, h, piece] = from_g.astype(jnp.bfloat16)
            dkv_send[1, h, piece] = from_y.astype(jnp.bfloat16)
        guarded(has_zout, lambda: send_dkv(0, h, zout))
        guarded(bent, lambda: send_dkv(1, h, across))

    def stage_return(h):
        send_dq(X, h)

    def stage_final(h):
        from_reached(dq_in, h, dq_rsem)
        total = dq_own[h]
        for n in (C, Y, X):
            total = total + dq_in[n, h].astype(jnp.float32)
        dq_out[0, 0, :, cols(h)] = total.T.astype(jnp.bfloat16)
        by_count(0, has_f, bent, lambda count: landed(dkv_in.at[pl.ds(0, count), h], dkv_rsem.at[h]))
        for piece, out in enumerate((dk_out, dv_out)):
            total = dkv_own[h, piece]
            for at in range(2):
                total = total + dkv_in[at, h, piece].astype(jnp.float32)
            out[0, 0, :, cols(h)] = total.astype(jnp.bfloat16)

    def stage_arrival(h):
        landed(fw.at[X, h], x_rsem.at[h])

        @pl.when(h + AHEAD < heads)
        def _():
            send_own(h + AHEAD)

    def stage_second_piece(h):
        @pl.when(h + AHEAD < heads)
        def _():
            send_x(h + AHEAD, 1)

    wait_load(AHEAD, heads, 1)
    stages = (
        (0, stage_arrival),
        (LAG_SCORES, stage_scores),
        (LAG_COMBINE, stage_combine),
        (0, stage_second_piece),
        (LAG_FINAL, stage_final),
        (LAG_RETURN, stage_return),
        (LAG_GRADS, stage_grads),
    )

    @pl.loop(0, heads + LAG_FINAL)
    def _(tick):
        @pl.when(tick == LAG_SCORES)
        def _():
            landed(bias_x, bias_rsem.at[1])

            @pl.when(straight)
            def _():
                landed(bias_in.at[pl.ds(1, 2)], bias_rsem.at[0])

            @pl.when(jnp.logical_not(straight))
            def _():
                landed(bias_in.at[pl.ds(1, 1)], bias_rsem.at[0])

        for lag, stage in stages:

            @pl.when((tick >= lag) & (tick < heads + lag))
            def _(lag=lag, stage=stage):
                stage(tick - lag)

    for n, condition in ((X, None), (C, None), (Y, has_y), (F, has_f)):
        guarded(condition, lambda n=n: sent(fw.at[OWN], fwd_ssem.at[n]))

    def wait_sends(n):
        sent(bias_out if n == X else bias_out.at[n], bias_ssem.at[n])
        sent(st_out.at[n], st_ssem.at[n])
        sent(fin_own, fin_ssem.at[n])
        sent(dq_send.at[n], dq_ssem.at[n])

    for n in (C, Y, X):
        guarded(reached[n], functools.partial(wait_sends, n))
    guarded(has_zout, lambda: sent(dkv_send.at[0], dkv_ssem.at[0]))
    guarded(bent, lambda: sent(dkv_send.at[1], dkv_ssem.at[1]))


def store(a, b, c, a_out, b_out, c_out, sems):
    pairs = ((a, a_out), (b, b_out), (c, c_out))
    copies = [pltpu.make_async_copy(x, y, sems.at[i]) for i, (x, y) in enumerate(pairs)]
    for copy in copies:
        copy.start()
    for copy in copies:
        copy.wait()


def body(slabs, bands, queries, key_states, value_states, grad_out, window):
    features = queries.shape[3]
    heads = features // HEAD_DIM
    f32, bf16 = jnp.float32, jnp.bfloat16
    dma = pltpu.SemaphoreType.DMA
    out = jax.ShapeDtypeStruct(queries.shape, bf16)
    anywhere = pl.BlockSpec(memory_space=pl.ANY)
    vmem = pl.BlockSpec(memory_space=pltpu.VMEM)
    macs = heads * 5 * 5 * BLOCK * BLOCK * HEAD_DIM
    outs = pl.pallas_call(
        functools.partial(kernel, slabs, bands, heads),
        out_shape=(pltpu.VMEM(queries.shape, bf16),) * 3,
        in_specs=[anywhere] * 5,
        out_specs=(vmem, vmem, vmem),
        scratch_shapes=[
            pltpu.SMEM(window.shape, jnp.int32),
            pltpu.VMEM((4, heads, 2, BLOCK, HEAD_DIM), bf16),
            pltpu.VMEM((3, heads, 2, BLOCK, HEAD_DIM), bf16),
            pltpu.VMEM((heads, BLOCK, 5 * BLOCK), f32),
            pltpu.VMEM((heads, BLOCK, 5 * BLOCK), f32),
            pltpu.VMEM((heads, 5, 1, BLOCK), f32),
            pltpu.VMEM((5, 2, 1, BLOCK), f32),
            pltpu.VMEM((3, 2, 1, BLOCK), f32),
            pltpu.VMEM((5, 2, 1, BLOCK), f32),
            pltpu.VMEM((heads, 3, 1, BLOCK), f32),
            pltpu.VMEM((4, heads, 3, 1, BLOCK), f32),
            pltpu.VMEM((4, heads, 3, 1, BLOCK), f32),
            pltpu.VMEM((heads, 3, 1, BLOCK), f32),
            pltpu.VMEM((4, heads, 3, 1, BLOCK), f32),
            pltpu.VMEM((heads, HEAD_DIM, BLOCK), f32),
            pltpu.VMEM((4, heads, HEAD_DIM, BLOCK), bf16),
            pltpu.VMEM((4, heads, HEAD_DIM, BLOCK), bf16),
            pltpu.VMEM((heads, 2, BLOCK, HEAD_DIM), f32),
            pltpu.VMEM((2, heads, 2, BLOCK, HEAD_DIM), bf16),
            pltpu.VMEM((2, heads, 2, BLOCK, HEAD_DIM), bf16),
            dma((3,)),
            dma((4,)),
            dma((2,)),
            dma((5,)),
            dma((heads,)),
            dma((heads,)),
            dma((4,)),
            dma((heads,)),
            dma((4,)),
            dma((heads,)),
            dma((4,)),
            dma((heads,)),
            dma((2,)),
            dma((heads,)),
        ],
        compiler_params=pltpu.CompilerParams(
            collective_id=0, has_side_effects=True, vmem_limit_bytes=58 << 20
        ),
        cost_estimate=pl.CostEstimate(
            flops=2 * macs,
            bytes_accessed=7 * BLOCK * features * 2,
            transcendentals=heads * 5 * BLOCK * BLOCK,
        ),
    )(queries, key_states, value_states, grad_out, window)

    return pl.pallas_call(
        store,
        out_shape=(out, out, out),
        in_specs=[vmem] * 3,
        out_specs=[anywhere] * 3,
        scratch_shapes=[dma((3,))],
        compiler_params=pltpu.CompilerParams(vmem_limit_bytes=8 << 20),
    )(*outs)


def solution(mesh):
    spec = P("tm", "space", None, None)
    return jax.shard_map(
        functools.partial(body, mesh.shape["tm"], mesh.shape["space"]),
        mesh=mesh,
        in_specs=(spec,) * 5,
        out_specs=(spec,) * 3,
        check_vma=False,
    )
```

```python
import functools
import itertools
import math

import jax
import jax.numpy as jnp
from jax import lax
from jax.experimental import pallas as pl
from jax.experimental.pallas import tpu as pltpu
from jax.sharding import PartitionSpec as P

MESH = pl.DeviceIdType.MESH
HEAD_DIM = 128
TILE_TOKENS = 64
BLOCK = 128
MASKED = -1e30
SCALE = HEAD_DIM ** (-0.5)
SCALE_LOG2E = SCALE * math.log2(math.e)

OWN, C, Y, X, F = range(5)
G, H = 1, 2
PAIRS = (OWN, C, X, Y, F)
AHEAD = 3
LAG_SCORES, LAG_GRADS, LAG_RETURN, LAG_FINAL = 1, 4, 8, 12


def kernel(
    slabs,
    bands,
    heads,
    q_hbm,
    k_hbm,
    v_hbm,
    g_hbm,
    window_hbm,
    dq_out,
    dk_out,
    dv_out,
    window,
    fw,
    kv,
    weight,
    gprob,
    tops,
    bias_out,
    bias_in,
    bias_x,
    st_out,
    st_in,
    dq_own,
    dq_send,
    dq_in,
    dkv_own,
    dkv_send,
    dkv_in,
    load_sem,
    bias_ssem,
    bias_rsem,
    fwd_ssem,
    x_rsem,
    arr_rsem,
    st_ssem,
    st_rsem,
    dq_ssem,
    dq_rsem,
    dkv_ssem,
    dkv_rsem,
):
    t = lax.axis_index("tm")
    b = lax.axis_index("space")
    tstep = 2 * lax.rem(t, 2) - 1
    bstep = 1 - 2 * lax.rem(b, 2)
    t_c, t_y = t - tstep, t + tstep
    b_x, b_f = b + bstep, b - bstep
    b_zout, b_zin = b + 2 * bstep, b - 2 * bstep
    has_y = (t_y >= 0) & (t_y < slabs)
    has_f = (b_f >= 0) & (b_f < bands)
    has_zout = (b_zout >= 0) & (b_zout < bands)
    bent = (t == slabs // 2 - 1) | (t == slabs // 2)
    straight = has_y & jnp.logical_not(bent)
    t_cy, t_yc = t - 2 * tstep, t + 2 * tstep
    c_bent = (t_c == slabs // 2 - 1) | (t_c == slabs // 2)
    c_straight = (t_cy >= 0) & (t_cy < slabs) & jnp.logical_not(c_bent)

    partner = {C: (t_c, b), Y: (t_y, b), X: (t, b_x)}
    reached = {C: None, Y: straight, X: None}
    across, zout, zin = (t_y, b_x), (t, b_zout), (t, b_zin)
    beside, c_y, y_c = (t_c, b_x), (t_cy, b), (t_yc, b)

    def guarded(condition, action):
        if condition is None:
            action()
        else:
            pl.when(condition)(action)

    def cols(h):
        return pl.ds(pl.multiple_of(h * HEAD_DIM, HEAD_DIM), HEAD_DIM)

    def start_load(h):
        sem = load_sem.at[jnp.where(h < AHEAD, 0, 1)]
        for src, dst in (
            (q_hbm, fw.at[OWN, h, 0]),
            (g_hbm, fw.at[OWN, h, 1]),
            (k_hbm, kv.at[OWN, h, 0]),
            (v_hbm, kv.at[OWN, h, 1]),
        ):
            pltpu.make_async_copy(src.at[0, 0, :, cols(h)], dst, sem).start()

    def wait_load(first, last, sem):
        span = pl.ds(first, last - first)
        both = fw.at[pl.ds(0, 2), span]
        pltpu.make_async_copy(both, both, load_sem.at[sem]).wait()

    window_load = pltpu.make_async_copy(window_hbm, window, load_sem.at[2])

    barrier = pltpu.get_barrier_semaphore()

    def greet(device):
        pl.semaphore_signal(barrier, inc=1, device_id=device, device_id_type=MESH)

    for device, condition in (
        (partner[X], None),
        (partner[C], None),
        (partner[Y], straight),
        (across, has_y),
        (beside, None),
        (c_y, c_straight),
        (y_c, straight),
        (zout, has_zout),
        (zin, has_f),
    ):
        guarded(condition, functools.partial(greet, device))

    @pl.loop(0, AHEAD)
    def _(h):
        start_load(h)

    window_load.start()
    count = 3 + has_y.astype(jnp.int32) + has_f.astype(jnp.int32) + has_zout.astype(jnp.int32)
    count = count + 2 * straight.astype(jnp.int32) + c_straight.astype(jnp.int32)
    pl.semaphore_wait(barrier, count)

    def remote(src, dst, send, recv, device):
        return pltpu.make_async_remote_copy(
            src_ref=src,
            dst_ref=dst,
            send_sem=send,
            recv_sem=recv,
            device_id=device,
            device_id_type=MESH,
        )

    def bias_copy(n):
        if n == X:
            return remote(bias_out, bias_x, bias_ssem.at[X], bias_rsem.at[1], partner[X])
        return remote(bias_out.at[n], bias_in.at[n], bias_ssem.at[n], bias_rsem.at[0], partner[n])

    def send_x(h, piece):
        remote(
            fw.at[OWN, h, piece],
            fw.at[X, h, piece],
            fwd_ssem.at[X],
            x_rsem.at[h],
            partner[X],
        ).start()

    def send_own(h):
        send_x(h, 0)
        send_rest(h)

    def send_rest(h):
        recv = arr_rsem.at[h]

        @pl.when(has_f)
        def _():
            remote(kv.at[OWN, h], kv.at[G, h], fwd_ssem.at[F], recv, zin).start()

        @pl.when(bent)
        def _():
            remote(kv.at[OWN, h], kv.at[H, h], fwd_ssem.at[Y], recv, across).start()

        @pl.when(straight)
        def _():
            remote(fw.at[OWN, h], fw.at[Y, h], fwd_ssem.at[Y], recv, partner[Y]).start()

        remote(fw.at[OWN, h], fw.at[C, h], fwd_ssem.at[C], recv, partner[C]).start()

    def send_st(n, at, device, group, h):
        remote(st_out.at[n, h], st_in.at[at, h], st_ssem.at[group], st_rsem.at[h], device).start()

    def send_parts(h):
        send_st(2, 1, partner[X], 0, h)
        send_st(0, 6, partner[X], 0, h)
        send_st(2, 4, beside, 0, h)
        send_st(1, 7, beside, 0, h)
        send_st(1, 0, partner[C], 0, h)
        send_st(0, 3, partner[C], 0, h)

        @pl.when(straight)
        def _():
            send_st(2, 11, across, 1, h)
            send_st(3, 8, across, 1, h)
            send_st(3, 2, partner[Y], 1, h)
            send_st(0, 9, partner[Y], 1, h)
            send_st(3, 5, y_c, 1, h)

        @pl.when(c_straight)
        def _():
            send_st(1, 10, c_y, 2, h)

    def send_dq(n, h):
        remote(
            dq_send.at[n, h], dq_in.at[n, h], dq_ssem.at[n], dq_rsem.at[h], partner[n]
        ).start()

    def send_dkv(at, h, device):
        remote(
            dkv_send.at[at, h], dkv_in.at[at, h], dkv_ssem.at[at], dkv_rsem.at[h], device
        ).start()

    def landed(span, sem):
        remote(span, span, fwd_ssem.at[OWN], sem, partner[C]).wait_recv()

    def sent(span, sem):
        remote(span, span, sem, x_rsem.at[0], partner[C]).wait_send()

    def by_count(least, first, second, act):
        for more, condition in (
            (2, first & second),
            (1, first != second),
            (0, jnp.logical_not(first | second)),
        ):
            if least + more:
                pl.when(condition)(functools.partial(act, least + more))

    def from_reached(buffer, h, sem):
        @pl.when(straight)
        def _():
            landed(buffer.at[pl.ds(1, 3), h], sem.at[h])

        @pl.when(jnp.logical_not(straight))
        def _():
            landed(buffer.at[pl.ds(1, 2), h], sem.at[h])

    wait_load(0, AHEAD, 0)

    @pl.loop(0, AHEAD)
    def _(h):
        send_x(h, 0)
        send_x(h, 1)
        send_rest(h)

    @pl.loop(AHEAD, heads)
    def _(h):
        start_load(h)

    window_load.wait()

    lane_tile = lax.broadcasted_iota(jnp.int32, (1, BLOCK), 1) // TILE_TOKENS
    present = {Y: has_y, F: has_f}
    dirs = {
        OWN: (0, 0),
        C: (-tstep, 0),
        Y: (tstep, 0),
        X: (0, bstep),
        F: (0, -bstep),
    }
    for n in (OWN, C, Y, X, F):
        dt, dr = dirs[n]
        for key_tile in range(2):
            row = None
            for query_tile in range(2):
                dc = key_tile - query_tile
                if n == OWN and dc == 0:
                    value = jnp.float32(0.0)
                else:
                    code = 9 * (dt + 1) + 3 * (dr + 1) + dc + 1
                    listed = window[0, 0, query_tile, code]
                    shown = listed == 1
                    if n in present:
                        shown = shown & present[n]
                    value = jnp.where(shown, 0.0, MASKED).astype(jnp.float32)
                part = jnp.full((1, BLOCK), value, jnp.float32)
                row = part if row is None else jnp.where(lane_tile == 0, row, part)
            bias_out[n, key_tile] = row

    for n in (X, C, Y):
        guarded(reached[n], lambda n=n: bias_copy(n).start())

    def blank_part(at, h):
        st_in[at, h, 0] = jnp.full((1, BLOCK), MASKED, jnp.float32)
        for row in (1, 2):
            st_in[at, h, row] = jnp.zeros((1, BLOCK), jnp.float32)

    @pl.when(jnp.logical_not(c_straight))
    def _():
        @pl.loop(0, heads)
        def _(h):
            blank_part(5, h)

    @pl.when(jnp.logical_not(straight))
    def _():
        bias_in[Y] = jnp.zeros_like(bias_in[Y])

        @pl.loop(0, heads)
        def _(h):
            fw[Y, h] = jnp.zeros(fw.shape[2:], fw.dtype)
            for at in (2, 8, 9, 10, 11):
                blank_part(at, h)
            dq_in[Y, h] = jnp.zeros(dq_in.shape[2:], dq_in.dtype)

    @pl.when(jnp.logical_not(has_zout))
    def _():
        @pl.loop(0, heads)
        def _(h):
            kv[G, h] = jnp.zeros(kv.shape[2:], kv.dtype)

    for at, condition in ((0, has_f), (1, bent)):

        @pl.when(jnp.logical_not(condition))
        def _(at=at):
            @pl.loop(0, heads)
            def _(h):
                dkv_in[at, h] = jnp.zeros(dkv_in.shape[2:], dkv_in.dtype)

    y_queries = jnp.where(bent, X, Y)
    y_keys = jnp.where(bent, H, OWN)

    def dot(a, b, a_dim, b_dim):
        return lax.dot_general(
            a, b, (((a_dim,), (b_dim,)), ((), ())), preferred_element_type=jnp.float32
        )

    def thrice(h, piece):
        return jnp.concatenate([fw[n, h, piece] for n in (OWN, C, X)], axis=0)

    def products(h, piece):
        return jnp.concatenate(
            [
                dot(kv[OWN, h, piece], thrice(h, piece), 1, 1),
                dot(kv[y_keys, h, piece], fw[y_queries, h, piece], 1, 1),
                dot(kv[G, h, piece], fw[X, h, piece], 1, 1),
            ],
            axis=1,
        )

    def split(row):
        return {n: row[:, i * BLOCK : (i + 1) * BLOCK] for i, n in enumerate(PAIRS)}

    def merged(parts):
        top = functools.reduce(jnp.maximum, [part[0] for part in parts])
        shares = [jnp.exp2((part[0] - top) * SCALE_LOG2E) for part in parts]
        total, mixed = (
            sum(share * part[at] for share, part in zip(shares, parts)) for at in (1, 2)
        )
        return top, total, mixed

    def stage_scores(h):
        by_count(1, has_y, has_zout, lambda count: landed(fw.at[pl.ds(0, count), h], arr_rsem.at[h]))
        masks = []
        for key_tile in range(2):
            y_mask = jnp.where(bent, bias_x[Y, key_tile], bias_in[Y, key_tile])
            rows = [bias_out[OWN, key_tile], bias_in[C, key_tile], bias_x[X, key_tile]]
            masks.append(jnp.concatenate(rows + [y_mask, bias_x[F, key_tile]], axis=1))
        scores = products(h, 0)
        scores = jnp.concatenate(
            [scores[:TILE_TOKENS] + masks[0], scores[TILE_TOKENS:] + masks[1]], axis=0
        )
        top = jnp.max(scores, axis=0, keepdims=True)
        powers = jnp.exp2((scores - top) * SCALE_LOG2E)
        weight[h] = powers
        total = jnp.sum(powers, axis=0, keepdims=True)
        grad_probs = products(h, 1)
        gprob[h] = grad_probs
        mixed = jnp.sum(powers * grad_probs, axis=0, keepdims=True)
        top, total, mixed = split(top), split(total), split(mixed)
        for i, n in enumerate(PAIRS):
            tops[h, i] = top[n]
        part = {n: (top[n], total[n], mixed[n]) for n in PAIRS}
        y_part = (jnp.where(bent, top[Y], MASKED),) + tuple(
            jnp.where(bent, row[Y], 0.0) for row in (total, mixed)
        )
        x_part = merged([part[X], part[F], y_part])
        for slot, rows in enumerate((part[OWN], part[C], x_part, part[Y])):
            for at in range(3):
                st_out[slot, h, at] = rows[at]
        send_parts(h)

    def stage_grads(h):
        for its, own in itertools.product((False, True), repeat=2):

            @pl.when((c_straight == its) & (straight == own))
            def _(its=its, own=own):
                landed(st_in.at[pl.ds(0, 6 + 5 * own + its), h], st_rsem.at[h])

        def side_by_side(ref, places, at):
            return jnp.concatenate([ref[place, h, at] for place in places], axis=1)

        parts = [tuple(side_by_side(st_out, range(4), at) for at in range(3))]
        for sender in range(3):
            places = range(sender, 12, 3)
            parts.append(tuple(side_by_side(st_in, places, at) for at in range(3)))
        top, total, mixed = merged(parts)
        inverse = 1.0 / total

        def for_pairs(row):
            x_row, y_row = row[:, 2 * BLOCK : 3 * BLOCK], row[:, 3 * BLOCK :]
            y_row = jnp.where(bent, x_row, y_row)
            return jnp.concatenate([row[:, : 3 * BLOCK], y_row, x_row], axis=1)

        top, inverse, delta = for_pairs(top), for_pairs(inverse), for_pairs(mixed * inverse)
        own_top = jnp.concatenate([tops[h, i] for i in range(5)], axis=1)
        factor = jnp.exp2((own_top - top) * SCALE_LOG2E) * inverse
        probs = weight[h] * factor
        grad_scores = (probs * ((gprob[h] - delta) * SCALE)).astype(jnp.bfloat16)
        probs = probs.astype(jnp.bfloat16)
        third, fourth = 3 * BLOCK, 4 * BLOCK
        lefts = (grad_scores, probs)
        for piece, left in enumerate(lefts):
            from_g = dot(left[:, fourth:], fw[X, h, piece], 1, 0)
            dkv_send[0, h, piece] = from_g.astype(jnp.bfloat16)
        guarded(has_zout, lambda: send_dkv(0, h, zout))
        for piece, left in enumerate(lefts):
            from_y = dot(left[:, third:fourth], fw[y_queries, h, piece], 1, 0)
            dkv_send[1, h, piece] = from_y.astype(jnp.bfloat16)
            dkv_own[h, piece] = jnp.where(bent, 0.0, from_y)
        guarded(bent, lambda: send_dkv(1, h, across))
        turned = dot(kv[OWN, h, 0], grad_scores[:, :third], 0, 0)
        y_turned = dot(kv[y_keys, h, 0], grad_scores[:, third:fourth], 0, 0)
        g_turned = dot(kv[G, h, 0], grad_scores[:, fourth:], 0, 0)
        dq_own[h] = turned[:, :BLOCK]
        dq_send[C, h] = turned[:, BLOCK : 2 * BLOCK].astype(jnp.bfloat16)
        dq_send[Y, h] = y_turned.astype(jnp.bfloat16)
        x_turned = turned[:, 2 * BLOCK :] + g_turned + jnp.where(bent, y_turned, 0.0)
        dq_send[X, h] = x_turned.astype(jnp.bfloat16)
        guarded(straight, lambda: send_dq(Y, h))
        send_dq(C, h)
        for piece, left in enumerate(lefts):
            own = dot(left[:, :third], thrice(h, piece), 1, 0)
            dkv_own[h, piece] = dkv_own[h, piece] + own

    def stage_return(h):
        send_dq(X, h)

    def stage_final(h):
        from_reached(dq_in, h, dq_rsem)
        total = dq_own[h]
        for n in (C, Y, X):
            total = total + dq_in[n, h].astype(jnp.float32)
        dq_out[0, 0, :, cols(h)] = total.T.astype(jnp.bfloat16)
        by_count(0, has_f, bent, lambda count: landed(dkv_in.at[pl.ds(0, count), h], dkv_rsem.at[h]))
        for piece, out in enumerate((dk_out, dv_out)):
            total = dkv_own[h, piece]
            for at in range(2):
                total = total + dkv_in[at, h, piece].astype(jnp.float32)
            out[0, 0, :, cols(h)] = total.astype(jnp.bfloat16)

    def stage_arrival(h):
        landed(fw.at[X, h], x_rsem.at[h])

        @pl.when(h + AHEAD < heads)
        def _():
            send_own(h + AHEAD)

    def stage_second_piece(h):
        @pl.when(h + AHEAD < heads)
        def _():
            send_x(h + AHEAD, 1)

    wait_load(AHEAD, heads, 1)
    stages = (
        (0, stage_arrival),
        (LAG_SCORES, stage_scores),
        (0, stage_second_piece),
        (LAG_FINAL, stage_final),
        (LAG_RETURN, stage_return),
        (LAG_GRADS, stage_grads),
    )

    @pl.loop(0, heads + LAG_FINAL)
    def _(tick):
        @pl.when(tick == LAG_SCORES)
        def _():
            landed(bias_x, bias_rsem.at[1])

            @pl.when(straight)
            def _():
                landed(bias_in.at[pl.ds(1, 2)], bias_rsem.at[0])

            @pl.when(jnp.logical_not(straight))
            def _():
                landed(bias_in.at[pl.ds(1, 1)], bias_rsem.at[0])

        for lag, stage in stages:

            @pl.when((tick >= lag) & (tick < heads + lag))
            def _(lag=lag, stage=stage):
                stage(tick - lag)

    for n, condition in ((X, None), (C, None), (Y, has_y), (F, has_f)):
        guarded(condition, lambda n=n: sent(fw.at[OWN], fwd_ssem.at[n]))

    def wait_sends(n):
        sent(bias_out if n == X else bias_out.at[n], bias_ssem.at[n])
        sent(dq_send.at[n], dq_ssem.at[n])

    for n in (C, Y, X):
        guarded(reached[n], functools.partial(wait_sends, n))
    for group, (parts, condition) in enumerate(((6, None), (5, straight), (1, c_straight))):
        guarded(
            condition,
            lambda group=group, parts=parts: sent(st_in.at[pl.ds(0, parts)], st_ssem.at[group]),
        )
    guarded(has_zout, lambda: sent(dkv_send.at[0], dkv_ssem.at[0]))
    guarded(bent, lambda: sent(dkv_send.at[1], dkv_ssem.at[1]))


def store(a, b, c, a_out, b_out, c_out, sems):
    pairs = ((a, a_out), (b, b_out), (c, c_out))
    copies = [pltpu.make_async_copy(x, y, sems.at[i]) for i, (x, y) in enumerate(pairs)]
    for copy in copies:
        copy.start()
    for copy in copies:
        copy.wait()


def body(slabs, bands, queries, key_states, value_states, grad_out, window):
    features = queries.shape[3]
    heads = features // HEAD_DIM
    f32, bf16 = jnp.float32, jnp.bfloat16
    dma = pltpu.SemaphoreType.DMA
    out = jax.ShapeDtypeStruct(queries.shape, bf16)
    anywhere = pl.BlockSpec(memory_space=pl.ANY)
    vmem = pl.BlockSpec(memory_space=pltpu.VMEM)
    macs = heads * 5 * 5 * BLOCK * BLOCK * HEAD_DIM
    outs = pl.pallas_call(
        functools.partial(kernel, slabs, bands, heads),
        out_shape=(pltpu.VMEM(queries.shape, bf16),) * 3,
        in_specs=[anywhere] * 5,
        out_specs=(vmem, vmem, vmem),
        scratch_shapes=[
            pltpu.SMEM(window.shape, jnp.int32),
            pltpu.VMEM((4, heads, 2, BLOCK, HEAD_DIM), bf16),
            pltpu.VMEM((3, heads, 2, BLOCK, HEAD_DIM), bf16),
            pltpu.VMEM((heads, BLOCK, 5 * BLOCK), f32),
            pltpu.VMEM((heads, BLOCK, 5 * BLOCK), f32),
            pltpu.VMEM((heads, 5, 1, BLOCK), f32),
            pltpu.VMEM((5, 2, 1, BLOCK), f32),
            pltpu.VMEM((3, 2, 1, BLOCK), f32),
            pltpu.VMEM((5, 2, 1, BLOCK), f32),
            pltpu.VMEM((4, heads, 3, 1, BLOCK), f32),
            pltpu.VMEM((12, heads, 3, 1, BLOCK), f32),
            pltpu.VMEM((heads, HEAD_DIM, BLOCK), f32),
            pltpu.VMEM((4, heads, HEAD_DIM, BLOCK), bf16),
            pltpu.VMEM((4, heads, HEAD_DIM, BLOCK), bf16),
            pltpu.VMEM((heads, 2, BLOCK, HEAD_DIM), f32),
            pltpu.VMEM((2, heads, 2, BLOCK, HEAD_DIM), bf16),
            pltpu.VMEM((2, heads, 2, BLOCK, HEAD_DIM), bf16),
            dma((3,)),
            dma((4,)),
            dma((2,)),
            dma((5,)),
            dma((heads,)),
            dma((heads,)),
            dma((3,)),
            dma((heads,)),
            dma((4,)),
            dma((heads,)),
            dma((2,)),
            dma((heads,)),
        ],
        compiler_params=pltpu.CompilerParams(
            collective_id=0, has_side_effects=True, vmem_limit_bytes=58 << 20
        ),
        cost_estimate=pl.CostEstimate(
            flops=2 * macs,
            bytes_accessed=7 * BLOCK * features * 2,
            transcendentals=heads * 5 * BLOCK * BLOCK,
        ),
    )(queries, key_states, value_states, grad_out, window)

    return pl.pallas_call(
        store,
        out_shape=(out, out, out),
        in_specs=[vmem] * 3,
        out_specs=[anywhere] * 3,
        scratch_shapes=[dma((3,))],
        compiler_params=pltpu.CompilerParams(vmem_limit_bytes=8 << 20),
    )(*outs)


def solution(mesh):
    spec = P("tm", "space", None, None)
    return jax.shard_map(
        functools.partial(body, mesh.shape["tm"], mesh.shape["space"]),
        mesh=mesh,
        in_specs=(spec,) * 5,
        out_specs=(spec,) * 3,
        check_vma=False,
    )
```

```python
import functools
import itertools
import math

import jax
import jax.numpy as jnp
from jax import lax
from jax.experimental import pallas as pl
from jax.experimental.pallas import tpu as pltpu
from jax.sharding import PartitionSpec as P

MESH = pl.DeviceIdType.MESH
HEAD_DIM = 128
TILE_TOKENS = 64
BLOCK = 128
MASKED = -1e30
SCALE = HEAD_DIM ** (-0.5)
SCALE_LOG2E = SCALE * math.log2(math.e)

OWN, C, Y, X, F = range(5)
G, H = 1, 2
PAIRS = (OWN, C, X, Y, F)
AHEAD = 3
LAG_SCORES, LAG_GRADS, LAG_RETURN, LAG_FINAL = 1, 4, 8, 12


def kernel(
    slabs,
    bands,
    heads,
    q_hbm,
    k_hbm,
    v_hbm,
    g_hbm,
    window_hbm,
    dq_out,
    dk_out,
    dv_out,
    window,
    fw,
    kv,
    weight,
    gprob,
    tops,
    bias_out,
    bias_in,
    bias_x,
    st_out,
    st_in,
    dq_own,
    dq_send,
    dq_in,
    dkv_own,
    dkv_send,
    dkv_in,
    load_sem,
    bias_ssem,
    bias_rsem,
    fwd_ssem,
    x_rsem,
    arr_rsem,
    st_ssem,
    st_rsem,
    dq_ssem,
    dq_rsem,
    dkv_ssem,
):
    t = lax.axis_index("tm")
    b = lax.axis_index("space")
    tstep = 2 * lax.rem(t, 2) - 1
    bstep = 1 - 2 * lax.rem(b, 2)
    t_c, t_y = t - tstep, t + tstep
    b_x, b_f = b + bstep, b - bstep
    b_zout, b_zin = b + 2 * bstep, b - 2 * bstep
    has_y = (t_y >= 0) & (t_y < slabs)
    has_f = (b_f >= 0) & (b_f < bands)
    has_zout = (b_zout >= 0) & (b_zout < bands)
    bent = (t == slabs // 2 - 1) | (t == slabs // 2)
    straight = has_y & jnp.logical_not(bent)
    t_cy, t_yc = t - 2 * tstep, t + 2 * tstep
    c_bent = (t_c == slabs // 2 - 1) | (t_c == slabs // 2)
    c_straight = (t_cy >= 0) & (t_cy < slabs) & jnp.logical_not(c_bent)

    partner = {C: (t_c, b), Y: (t_y, b), X: (t, b_x)}
    reached = {C: None, Y: straight, X: None}
    across, zout, zin = (t_y, b_x), (t, b_zout), (t, b_zin)
    beside, c_y, y_c = (t_c, b_x), (t_cy, b), (t_yc, b)

    def guarded(condition, action):
        if condition is None:
            action()
        else:
            pl.when(condition)(action)

    def cols(h):
        return pl.ds(pl.multiple_of(h * HEAD_DIM, HEAD_DIM), HEAD_DIM)

    def start_load(h):
        sem = load_sem.at[jnp.where(h < AHEAD, 0, 1)]
        for src, dst in (
            (q_hbm, fw.at[OWN, h, 0]),
            (g_hbm, fw.at[OWN, h, 1]),
            (k_hbm, kv.at[OWN, h, 0]),
            (v_hbm, kv.at[OWN, h, 1]),
        ):
            pltpu.make_async_copy(src.at[0, 0, :, cols(h)], dst, sem).start()

    def wait_load(first, last, sem):
        span = pl.ds(first, last - first)
        both = fw.at[pl.ds(0, 2), span]
        pltpu.make_async_copy(both, both, load_sem.at[sem]).wait()

    window_load = pltpu.make_async_copy(window_hbm, window, load_sem.at[2])

    barrier = pltpu.get_barrier_semaphore()

    def greet(device):
        pl.semaphore_signal(barrier, inc=1, device_id=device, device_id_type=MESH)

    for device, condition in (
        (partner[X], None),
        (partner[C], None),
        (partner[Y], straight),
        (across, has_y),
        (beside, None),
        (c_y, c_straight),
        (y_c, straight),
        (zout, has_zout),
        (zin, has_f),
    ):
        guarded(condition, functools.partial(greet, device))

    @pl.loop(0, AHEAD)
    def _(h):
        start_load(h)

    window_load.start()
    count = 3 + has_y.astype(jnp.int32) + has_f.astype(jnp.int32) + has_zout.astype(jnp.int32)
    count = count + 2 * straight.astype(jnp.int32) + c_straight.astype(jnp.int32)
    pl.semaphore_wait(barrier, count)

    def remote(src, dst, send, recv, device):
        return pltpu.make_async_remote_copy(
            src_ref=src,
            dst_ref=dst,
            send_sem=send,
            recv_sem=recv,
            device_id=device,
            device_id_type=MESH,
        )

    def bias_copy(n):
        if n == X:
            return remote(bias_out, bias_x, bias_ssem.at[X], bias_rsem.at[1], partner[X])
        return remote(bias_out.at[n], bias_in.at[n], bias_ssem.at[n], bias_rsem.at[0], partner[n])

    def send_x(h, piece):
        remote(
            fw.at[OWN, h, piece],
            fw.at[X, h, piece],
            fwd_ssem.at[X],
            x_rsem.at[h],
            partner[X],
        ).start()

    def send_own(h):
        send_x(h, 0)
        send_rest(h)

    def send_rest(h):
        recv = arr_rsem.at[h]

        @pl.when(has_f)
        def _():
            remote(kv.at[OWN, h], kv.at[G, h], fwd_ssem.at[F], recv, zin).start()

        @pl.when(bent)
        def _():
            remote(kv.at[OWN, h], kv.at[H, h], fwd_ssem.at[Y], recv, across).start()

        @pl.when(straight)
        def _():
            remote(fw.at[OWN, h], fw.at[Y, h], fwd_ssem.at[Y], recv, partner[Y]).start()

        remote(fw.at[OWN, h], fw.at[C, h], fwd_ssem.at[C], recv, partner[C]).start()

    def send_st(n, at, device, group, h):
        remote(st_out.at[n, h], st_in.at[at, h], st_ssem.at[group], st_rsem.at[h], device).start()

    def send_parts(h):
        send_st(2, 1, partner[X], 0, h)
        send_st(0, 6, partner[X], 0, h)
        send_st(2, 4, beside, 0, h)
        send_st(1, 7, beside, 0, h)
        send_st(1, 0, partner[C], 0, h)
        send_st(0, 3, partner[C], 0, h)

        @pl.when(straight)
        def _():
            send_st(2, 11, across, 1, h)
            send_st(3, 8, across, 1, h)
            send_st(3, 2, partner[Y], 1, h)
            send_st(0, 9, partner[Y], 1, h)
            send_st(3, 5, y_c, 1, h)

        @pl.when(c_straight)
        def _():
            send_st(1, 10, c_y, 2, h)

    def send_dq(n, h):
        remote(
            dq_send.at[n, h], dq_in.at[n, h], dq_ssem.at[n], dq_rsem.at[h], partner[n]
        ).start()

    def send_dkv(at, h, device):
        remote(
            dkv_send.at[at, h], dkv_in.at[at, h], dkv_ssem.at[at], dq_rsem.at[h], device
        ).start()

    def landed(span, sem):
        remote(span, span, fwd_ssem.at[OWN], sem, partner[C]).wait_recv()

    def sent(span, sem):
        remote(span, span, sem, x_rsem.at[0], partner[C]).wait_send()

    def by_count(least, first, second, act):
        for more, condition in (
            (2, first & second),
            (1, first != second),
            (0, jnp.logical_not(first | second)),
        ):
            if least + more:
                pl.when(condition)(functools.partial(act, least + more))

    def from_reached(buffer, h, sem):
        @pl.when(straight)
        def _():
            landed(buffer.at[pl.ds(1, 3), h], sem.at[h])

        @pl.when(jnp.logical_not(straight))
        def _():
            landed(buffer.at[pl.ds(1, 2), h], sem.at[h])

    wait_load(0, AHEAD, 0)

    @pl.loop(0, AHEAD)
    def _(h):
        send_x(h, 0)
        send_x(h, 1)
        send_rest(h)

    @pl.loop(AHEAD, heads)
    def _(h):
        start_load(h)

    window_load.wait()

    lane_tile = lax.broadcasted_iota(jnp.int32, (1, BLOCK), 1) // TILE_TOKENS
    present = {Y: has_y, F: has_f}
    dirs = {
        OWN: (0, 0),
        C: (-tstep, 0),
        Y: (tstep, 0),
        X: (0, bstep),
        F: (0, -bstep),
    }
    for n in (OWN, C, Y, X, F):
        dt, dr = dirs[n]
        for key_tile in range(2):
            row = None
            for query_tile in range(2):
                dc = key_tile - query_tile
                if n == OWN and dc == 0:
                    value = jnp.float32(0.0)
                else:
                    code = 9 * (dt + 1) + 3 * (dr + 1) + dc + 1
                    listed = window[0, 0, query_tile, code]
                    shown = listed == 1
                    if n in present:
                        shown = shown & present[n]
                    value = jnp.where(shown, 0.0, MASKED).astype(jnp.float32)
                part = jnp.full((1, BLOCK), value, jnp.float32)
                row = part if row is None else jnp.where(lane_tile == 0, row, part)
            bias_out[n, key_tile] = row

    for n in (X, C, Y):
        guarded(reached[n], lambda n=n: bias_copy(n).start())

    def blank_part(at, h):
        st_in[at, h, 0] = jnp.full((1, BLOCK), MASKED, jnp.float32)
        for row in (1, 2):
            st_in[at, h, row] = jnp.zeros((1, BLOCK), jnp.float32)

    @pl.when(jnp.logical_not(c_straight))
    def _():
        @pl.loop(0, heads)
        def _(h):
            blank_part(5, h)

    @pl.when(jnp.logical_not(straight))
    def _():
        bias_in[Y] = jnp.zeros_like(bias_in[Y])

        @pl.loop(0, heads)
        def _(h):
            fw[Y, h] = jnp.zeros(fw.shape[2:], fw.dtype)
            for at in (2, 8, 9, 10, 11):
                blank_part(at, h)
            dq_in[Y, h] = jnp.zeros(dq_in.shape[2:], dq_in.dtype)

    @pl.when(jnp.logical_not(has_zout))
    def _():
        @pl.loop(0, heads)
        def _(h):
            kv[G, h] = jnp.zeros(kv.shape[2:], kv.dtype)

    for at, condition in ((0, has_f), (1, bent)):

        @pl.when(jnp.logical_not(condition))
        def _(at=at):
            @pl.loop(0, heads)
            def _(h):
                dkv_in[at, h] = jnp.zeros(dkv_in.shape[2:], dkv_in.dtype)

    y_queries = jnp.where(bent, X, Y)
    y_keys = jnp.where(bent, H, OWN)

    def dot(a, b, a_dim, b_dim):
        return lax.dot_general(
            a, b, (((a_dim,), (b_dim,)), ((), ())), preferred_element_type=jnp.float32
        )

    def thrice(h, piece):
        return jnp.concatenate([fw[n, h, piece] for n in (OWN, C, X)], axis=0)

    def products(h, piece):
        return jnp.concatenate(
            [
                dot(kv[OWN, h, piece], thrice(h, piece), 1, 1),
                dot(kv[y_keys, h, piece], fw[y_queries, h, piece], 1, 1),
                dot(kv[G, h, piece], fw[X, h, piece], 1, 1),
            ],
            axis=1,
        )

    def split(row):
        return {n: row[:, i * BLOCK : (i + 1) * BLOCK] for i, n in enumerate(PAIRS)}

    def merged(parts):
        top = functools.reduce(jnp.maximum, [part[0] for part in parts])
        shares = [jnp.exp2((part[0] - top) * SCALE_LOG2E) for part in parts]
        total, mixed = (
            sum(share * part[at] for share, part in zip(shares, parts)) for at in (1, 2)
        )
        return top, total, mixed

    def stage_scores(h):
        by_count(1, has_y, has_zout, lambda count: landed(fw.at[pl.ds(0, count), h], arr_rsem.at[h]))
        masks = []
        for key_tile in range(2):
            y_mask = jnp.where(bent, bias_x[Y, key_tile], bias_in[Y, key_tile])
            rows = [bias_out[OWN, key_tile], bias_in[C, key_tile], bias_x[X, key_tile]]
            masks.append(jnp.concatenate(rows + [y_mask, bias_x[F, key_tile]], axis=1))
        scores = products(h, 0)
        scores = jnp.concatenate(
            [scores[:TILE_TOKENS] + masks[0], scores[TILE_TOKENS:] + masks[1]], axis=0
        )
        top = jnp.max(scores, axis=0, keepdims=True)
        powers = jnp.exp2((scores - top) * SCALE_LOG2E)
        weight[h] = powers
        total = jnp.sum(powers, axis=0, keepdims=True)
        grad_probs = products(h, 1)
        gprob[h] = grad_probs
        mixed = jnp.sum(powers * grad_probs, axis=0, keepdims=True)
        top, total, mixed = split(top), split(total), split(mixed)
        for i, n in enumerate(PAIRS):
            tops[h, i] = top[n]
        part = {n: (top[n], total[n], mixed[n]) for n in PAIRS}
        y_part = (jnp.where(bent, top[Y], MASKED),) + tuple(
            jnp.where(bent, row[Y], 0.0) for row in (total, mixed)
        )
        x_part = merged([part[X], part[F], y_part])
        for slot, rows in enumerate((part[OWN], part[C], x_part, part[Y])):
            for at in range(3):
                st_out[slot, h, at] = rows[at]
        send_parts(h)

    def stage_grads(h):
        for its, own in itertools.product((False, True), repeat=2):

            @pl.when((c_straight == its) & (straight == own))
            def _(its=its, own=own):
                landed(st_in.at[pl.ds(0, 6 + 5 * own + its), h], st_rsem.at[h])

        def side_by_side(ref, places, at):
            return jnp.concatenate([ref[place, h, at] for place in places], axis=1)

        parts = [tuple(side_by_side(st_out, range(4), at) for at in range(3))]
        for sender in range(3):
            places = range(sender, 12, 3)
            parts.append(tuple(side_by_side(st_in, places, at) for at in range(3)))
        top, total, mixed = merged(parts)
        inverse = 1.0 / total

        def for_pairs(row):
            x_row, y_row = row[:, 2 * BLOCK : 3 * BLOCK], row[:, 3 * BLOCK :]
            y_row = jnp.where(bent, x_row, y_row)
            return jnp.concatenate([row[:, : 3 * BLOCK], y_row, x_row], axis=1)

        top, inverse, delta = for_pairs(top), for_pairs(inverse), for_pairs(mixed * inverse)
        own_top = jnp.concatenate([tops[h, i] for i in range(5)], axis=1)
        factor = jnp.exp2((own_top - top) * SCALE_LOG2E) * inverse
        probs = weight[h] * factor
        grad_scores = (probs * ((gprob[h] - delta) * SCALE)).astype(jnp.bfloat16)
        probs = probs.astype(jnp.bfloat16)
        third, fourth = 3 * BLOCK, 4 * BLOCK
        lefts = (grad_scores, probs)
        for piece, left in enumerate(lefts):
            from_g = dot(left[:, fourth:], fw[X, h, piece], 1, 0)
            dkv_send[0, h, piece] = from_g.astype(jnp.bfloat16)
        guarded(has_zout, lambda: send_dkv(0, h, zout))
        for piece, left in enumerate(lefts):
            from_y = dot(left[:, third:fourth], fw[y_queries, h, piece], 1, 0)
            dkv_send[1, h, piece] = from_y.astype(jnp.bfloat16)
            dkv_own[h, piece] = jnp.where(bent, 0.0, from_y)
        guarded(bent, lambda: send_dkv(1, h, across))
        turned = dot(kv[OWN, h, 0], grad_scores[:, :third], 0, 0)
        y_turned = dot(kv[y_keys, h, 0], grad_scores[:, third:fourth], 0, 0)
        g_turned = dot(kv[G, h, 0], grad_scores[:, fourth:], 0, 0)
        dq_own[h] = turned[:, :BLOCK]
        dq_send[C, h] = turned[:, BLOCK : 2 * BLOCK].astype(jnp.bfloat16)
        dq_send[Y, h] = y_turned.astype(jnp.bfloat16)
        x_turned = turned[:, 2 * BLOCK :] + g_turned + jnp.where(bent, y_turned, 0.0)
        dq_send[X, h] = x_turned.astype(jnp.bfloat16)
        guarded(straight, lambda: send_dq(Y, h))
        send_dq(C, h)
        for piece, left in enumerate(lefts):
            own = dot(left[:, :third], thrice(h, piece), 1, 0)
            dkv_own[h, piece] = dkv_own[h, piece] + own

    def stage_return(h):
        send_dq(X, h)

    def stage_final(h):
        for more, terms in itertools.product((2, 3), range(3)):
            one, two = has_f != bent, has_f & bent
            pairs = (jnp.logical_not(has_f | bent), one, two)[terms]

            @pl.when(pairs & (straight == (more == 3)))
            def _(count=more + 2 * terms):
                landed(fw.at[0, pl.ds(0, count), 0], dq_rsem.at[h])

        total = dq_own[h]
        for n in (C, Y, X):
            total = total + dq_in[n, h].astype(jnp.float32)
        dq_out[0, 0, :, cols(h)] = total.T.astype(jnp.bfloat16)
        for piece, out in enumerate((dk_out, dv_out)):
            total = dkv_own[h, piece]
            for at in range(2):
                total = total + dkv_in[at, h, piece].astype(jnp.float32)
            out[0, 0, :, cols(h)] = total.astype(jnp.bfloat16)

    def stage_arrival(h):
        landed(fw.at[X, h], x_rsem.at[h])

        @pl.when(h + AHEAD < heads)
        def _():
            send_own(h + AHEAD)

    def stage_second_piece(h):
        @pl.when(h + AHEAD < heads)
        def _():
            send_x(h + AHEAD, 1)

    wait_load(AHEAD, heads, 1)
    stages = (
        (0, stage_arrival),
        (0, stage_second_piece),
        (LAG_SCORES, stage_scores),
        (LAG_FINAL, stage_final),
        (LAG_RETURN, stage_return),
        (LAG_GRADS, stage_grads),
    )

    @pl.loop(0, heads + LAG_FINAL)
    def _(tick):
        @pl.when(tick == LAG_SCORES)
        def _():
            landed(bias_x, bias_rsem.at[1])

            @pl.when(straight)
            def _():
                landed(bias_in.at[pl.ds(1, 2)], bias_rsem.at[0])

            @pl.when(jnp.logical_not(straight))
            def _():
                landed(bias_in.at[pl.ds(1, 1)], bias_rsem.at[0])

        for lag, stage in stages:

            @pl.when((tick >= lag) & (tick < heads + lag))
            def _(lag=lag, stage=stage):
                stage(tick - lag)

    for n, condition in ((X, None), (C, None), (Y, has_y), (F, has_f)):
        guarded(condition, lambda n=n: sent(fw.at[OWN], fwd_ssem.at[n]))

    def wait_sends(n):
        sent(bias_out if n == X else bias_out.at[n], bias_ssem.at[n])
        sent(dq_send.at[n], dq_ssem.at[n])

    for n in (C, Y, X):
        guarded(reached[n], functools.partial(wait_sends, n))
    for group, (parts, condition) in enumerate(((6, None), (5, straight), (1, c_straight))):
        guarded(
            condition,
            lambda group=group, parts=parts: sent(st_in.at[pl.ds(0, parts)], st_ssem.at[group]),
        )
    guarded(has_zout, lambda: sent(dkv_send.at[0], dkv_ssem.at[0]))
    guarded(bent, lambda: sent(dkv_send.at[1], dkv_ssem.at[1]))


def store(a, b, c, a_out, b_out, c_out, sems):
    pairs = ((a, a_out), (b, b_out), (c, c_out))
    copies = [pltpu.make_async_copy(x, y, sems.at[i]) for i, (x, y) in enumerate(pairs)]
    for copy in copies:
        copy.start()
    for copy in copies:
        copy.wait()


def body(slabs, bands, queries, key_states, value_states, grad_out, window):
    features = queries.shape[3]
    heads = features // HEAD_DIM
    f32, bf16 = jnp.float32, jnp.bfloat16
    dma = pltpu.SemaphoreType.DMA
    out = jax.ShapeDtypeStruct(queries.shape, bf16)
    anywhere = pl.BlockSpec(memory_space=pl.ANY)
    vmem = pl.BlockSpec(memory_space=pltpu.VMEM)
    macs = heads * 5 * 5 * BLOCK * BLOCK * HEAD_DIM
    outs = pl.pallas_call(
        functools.partial(kernel, slabs, bands, heads),
        out_shape=(pltpu.VMEM(queries.shape, bf16),) * 3,
        in_specs=[anywhere] * 5,
        out_specs=(vmem, vmem, vmem),
        scratch_shapes=[
            pltpu.SMEM(window.shape, jnp.int32),
            pltpu.VMEM((4, heads, 2, BLOCK, HEAD_DIM), bf16),
            pltpu.VMEM((3, heads, 2, BLOCK, HEAD_DIM), bf16),
            pltpu.VMEM((heads, BLOCK, 5 * BLOCK), f32),
            pltpu.VMEM((heads, BLOCK, 5 * BLOCK), f32),
            pltpu.VMEM((heads, 5, 1, BLOCK), f32),
            pltpu.VMEM((5, 2, 1, BLOCK), f32),
            pltpu.VMEM((3, 2, 1, BLOCK), f32),
            pltpu.VMEM((5, 2, 1, BLOCK), f32),
            pltpu.VMEM((4, heads, 3, 1, BLOCK), f32),
            pltpu.VMEM((12, heads, 3, 1, BLOCK), f32),
            pltpu.VMEM((heads, HEAD_DIM, BLOCK), f32),
            pltpu.VMEM((4, heads, HEAD_DIM, BLOCK), bf16),
            pltpu.VMEM((4, heads, HEAD_DIM, BLOCK), bf16),
            pltpu.VMEM((heads, 2, BLOCK, HEAD_DIM), f32),
            pltpu.VMEM((2, heads, 2, BLOCK, HEAD_DIM), bf16),
            pltpu.VMEM((2, heads, 2, BLOCK, HEAD_DIM), bf16),
            dma((3,)),
            dma((4,)),
            dma((2,)),
            dma((5,)),
            dma((heads,)),
            dma((heads,)),
            dma((3,)),
            dma((heads,)),
            dma((4,)),
            dma((heads,)),
            dma((2,)),
        ],
        compiler_params=pltpu.CompilerParams(
            collective_id=0, has_side_effects=True, vmem_limit_bytes=58 << 20
        ),
        cost_estimate=pl.CostEstimate(
            flops=2 * macs,
            bytes_accessed=7 * BLOCK * features * 2,
            transcendentals=heads * 5 * BLOCK * BLOCK,
        ),
    )(queries, key_states, value_states, grad_out, window)

    return pl.pallas_call(
        store,
        out_shape=(out, out, out),
        in_specs=[vmem] * 3,
        out_specs=[anywhere] * 3,
        scratch_shapes=[dma((3,))],
        compiler_params=pltpu.CompilerParams(vmem_limit_bytes=8 << 20),
    )(*outs)


def solution(mesh):
    spec = P("tm", "space", None, None)
    return jax.shard_map(
        functools.partial(body, mesh.shape["tm"], mesh.shape["space"]),
        mesh=mesh,
        in_specs=(spec,) * 5,
        out_specs=(spec,) * 3,
        check_vma=False,
    )
```
